32 devices in a mesh: dp: 8 (over z, x), tensor: 4 (over y, core).
Axes of the slice: x: 2, y: 2, z: 4, core: 2. Of those that a mesh axis runs over, the one named last changes fastest.
Arguments:
- tokens: bfloat16 [24576, 768], P('dp'), may hold values from -6 to 6
- ln1_gain: bfloat16 [768], replicated, may hold values from 0.25 to 1.75
- ln1_bias: bfloat16 [768], replicated, may hold values from -1.75 to 1.75
- ln2_gain: bfloat16 [768], replicated, may hold values from 0.25 to 1.75
- ln2_bias: bfloat16 [768], replicated, may hold values from -1.75 to 1.75
- qkv_weight: bfloat16 [768, 12, 192], P(None, 'tensor'), may hold values from -0.21875 to 0.21875
- qkv_bias: bfloat16 [12, 192], P('tensor'), may hold values from -1.75 to 1.75
- dense_weight: bfloat16 [768, 768], P('tensor'), may hold values from -1.75 to 1.75
- dense_bias: bfloat16 [768], replicated, may hold values from -1.75 to 1.75
- fc_weight: bfloat16 [768, 3072], P(None, 'tensor'), may hold values from -0.21875 to 0.21875
- fc_bias: bfloat16 [3072], P('tensor'), may hold values from -1.75 to 1.75
- proj_weight: bfloat16 [3072, 768], P('tensor'), may hold values from -0.109375 to 0.109375
- proj_bias: bfloat16 [768], replicated, may hold values from -1.75 to 1.75
- cotangent: bfloat16 [24576, 768], P('dp'), may hold values from -6 to 6
Outputs:
- block_out: bfloat16 [24576, 768], P('dp')
- input_grad: float32 [24576, 768], P('dp')
- ln1_gain_grad: float32 [768], replicated
- ln1_bias_grad: float32 [768], replicated
- ln2_gain_grad: float32 [768], replicated
- ln2_bias_grad: float32 [768], replicated
- qkv_weight_grad: float32 [768, 12, 192], P(None, 'tensor')
- qkv_bias_grad: float32 [12, 192], P('tensor')
- dense_weight_grad: float32 [768, 768], P('tensor')
- dense_bias_grad: float32 [768], replicated
- fc_weight_grad: float32 [768, 3072], P(None, 'tensor')
- fc_bias_grad: float32 [3072], P('tensor')
- proj_weight_grad: float32 [3072, 768], P('tensor')
- proj_bias_grad: float32 [768], replicated
The draws below stay inside these ranges and needn't reach their ends.
All inputs are finite; a program needn't handle non-finite values.
Results may differ from the reference program's by a relative error of at most 0.012.
The reference program's roundings to bfloat16 on the way count: a program that leaves them out, or rounds other values in their place, can miss the bound.
Values may be sent and summed in bfloat16 or wider, within the bound.
No kernel may reach another device: no remote copies, remote signals or barrier semaphores. Data moves between devices by JAX's collectives and lax.ppermute only.
A program may use at most 192 MiB of HBM per device.

```python
import math
import jax
import jax.numpy as jnp
from jax import lax

D = 768
HEADS = 12
HEAD = 64
FF = 3072
ROT = 16
LEN = 1024
TOKENS = 24576


def steps_of(rng, dims, pieces, low, largest):
    def one(dim, blocks):
        heights = jax.random.uniform(jax.random.fold_in(jax.random.fold_in(rng, 6), dim), (blocks,), jnp.float32, low / len(pieces), largest / len(pieces))
        return jnp.repeat(jnp.exp(heights), dims[dim] // blocks).reshape((-1,) + (1,) * (len(dims) - dim - 1))

    level = one(*pieces[0])
    for cut in pieces[1:]:
        level = level * one(*cut)
    return level


def noise(rng, dims, deviation, bound, pieces=(), dtype=jnp.bfloat16):
    drawn = deviation * jax.random.normal(rng, dims, jnp.float32)
    if pieces:
        drawn = drawn * steps_of(rng, dims, pieces, -0.22, 0.18)
    return jnp.clip(drawn, -bound, bound).astype(dtype)


def setup_inputs(seed: int = 0) -> dict:
    seeds = jax.random.split(jax.random.key(seed), 15)
    tokens = noise(seeds[0], (TOKENS, D), 1.0, 6.0, ((0, 8),))
    ln1_gain = jnp.clip(1.0 + 0.15 * jax.random.normal(seeds[1], (D,), jnp.float32), 0.25, 1.75).astype(jnp.bfloat16)
    ln1_bias = noise(seeds[2], (D,), 0.3, 1.75)
    ln2_gain = jnp.clip(1.0 + 0.15 * jax.random.normal(seeds[3], (D,), jnp.float32), 0.25, 1.75).astype(jnp.bfloat16)
    ln2_bias = noise(seeds[4], (D,), 0.3, 1.75)
    qkv_weight = noise(seeds[5], (D, HEADS, 3 * HEAD), D ** -0.5, 0.21875, ((1, 4),))
    qkv_bias = noise(seeds[6], (HEADS, 3 * HEAD), 0.3, 1.75, ((0, 4),))
    dense_weight = noise(seeds[7], (D, D), (D // 64) ** -0.5, 1.75, ((0, 4),))
    dense_bias = noise(seeds[8], (D,), 0.3, 1.75)
    fc_weight = noise(seeds[9], (D, FF), D ** -0.5, 0.21875, ((1, 4),))
    fc_bias = noise(seeds[10], (FF,), 0.3, 1.75, ((0, 4),))
    proj_weight = noise(seeds[11], (FF, D), FF ** -0.5, 0.109375, ((0, 4),))
    proj_bias = noise(seeds[12], (D,), 0.3, 1.75)
    cotangent = noise(seeds[13], (TOKENS, D), 1.0, 6.0, ((0, 8),))
    return dict(tokens=tokens, ln1_gain=ln1_gain, ln1_bias=ln1_bias, ln2_gain=ln2_gain, ln2_bias=ln2_bias, qkv_weight=qkv_weight, qkv_bias=qkv_bias, dense_weight=dense_weight, dense_bias=dense_bias, fc_weight=fc_weight, fc_bias=fc_bias, proj_weight=proj_weight, proj_bias=proj_bias, cotangent=cotangent)


@jax.custom_vjp
def low(v):
    return lax.optimization_barrier(v.astype(jnp.bfloat16)).astype(jnp.float32)

@jax.custom_vjp
def low_back(v):
    return v

def low_keep(v):
    return (low(v), None)

def low_pass(kept, grad):
    return (grad,)

def back_keep(v):
    return (v, None)

def back_low(kept, grad):
    return (low(grad),)
low.defvjp(low_keep, low_pass)
low_back.defvjp(back_keep, back_low)
EPSILON = 1e-05
ROTARY_BASE = 10000.0
MASKED = -1e+30

def norm_rows(rows, gain, shift):
    center = lax.optimization_barrier(jnp.mean(rows, axis=-1, keepdims=True))
    centred = rows - center
    spread = lax.optimization_barrier(jnp.mean(centred * centred, axis=-1, keepdims=True))
    return centred * lax.rsqrt(spread + EPSILON) * gain + shift

def rotate(block, rotary):
    length = block.shape[-3]
    half = rotary // 2
    position = jnp.arange(length).astype(jnp.float32)
    inverse = ROTARY_BASE ** (-(jnp.arange(half).astype(jnp.float32) * 2.0) / rotary)
    angle = position[:, None] * inverse[None, :]
    cosine = jnp.cos(angle)[:, None, :]
    sine = jnp.sin(angle)[:, None, :]
    first = block[..., :half]
    second = block[..., half:rotary]
    return jnp.concatenate([first * cosine - second * sine, second * cosine + first * sine, block[..., rotary:]], axis=-1)

def layer(rows, params):
    ln1_gain, ln1_bias, ln2_gain, ln2_bias, qkv_weight, qkv_bias, dense_weight, dense_bias, fc_weight, fc_bias, proj_weight, proj_bias = params
    highest = lax.Precision.HIGHEST
    normed_one = low(norm_rows(rows, ln1_gain, ln1_bias))
    normed_two = low(norm_rows(rows, ln2_gain, ln2_bias))
    mixed = jnp.dot(normed_one, qkv_weight.reshape(D, HEADS * 3 * HEAD), precision=highest)
    mixed = low_back(mixed + qkv_bias.reshape(HEADS * 3 * HEAD)).reshape(LEN, HEADS, 3 * HEAD)
    queries = low(rotate(mixed[..., :HEAD], ROT))
    keys = low(rotate(mixed[..., HEAD:2 * HEAD], ROT))
    values = low(mixed[..., 2 * HEAD:])
    scale = 1.0 / math.sqrt(HEAD)
    scores = low_back(jnp.einsum('qhd,khd->hqk', queries, keys, precision=highest) * scale)
    position = jnp.arange(LEN)
    scores = jnp.where(position[None, :] <= position[:, None], scores, MASKED)
    probs = low(jax.nn.softmax(scores, axis=-1))
    context = jnp.einsum('hqk,khd->qhd', probs, values, precision=highest)
    context = low(low_back(context)).reshape(LEN, D)
    attention = jnp.dot(context, dense_weight, precision=highest) + dense_bias
    hidden = low_back(jnp.dot(normed_two, fc_weight, precision=highest) + fc_bias)
    activated = low(jax.nn.gelu(hidden, approximate=False))
    feed = jnp.dot(activated, proj_weight, precision=highest) + proj_bias
    return rows + attention + feed

def reference(tokens, ln1_gain, ln1_bias, ln2_gain, ln2_bias, qkv_weight, qkv_bias, dense_weight, dense_bias, fc_weight, fc_bias, proj_weight, proj_bias, cotangent):
    params = tuple((item.astype(jnp.float32) for item in (ln1_gain, ln1_bias, ln2_gain, ln2_bias, qkv_weight, qkv_bias, dense_weight, dense_bias, fc_weight, fc_bias, proj_weight, proj_bias)))
    sequences = tokens.astype(jnp.float32).reshape(-1, LEN, D)
    upstream = cotangent.astype(jnp.float32).reshape(-1, LEN, D)
    zeros = jax.tree.map(jnp.zeros_like, params)

    def step(totals, item):
        rows, grads = item
        result, pull = jax.vjp(layer, rows, params)
        drows, dparams = pull(grads)
        return (jax.tree.map(jnp.add, totals, dparams), (result.astype(jnp.bfloat16), drows))
    totals, (results, drows) = lax.scan(step, zeros, (sequences, upstream))
    block_out = results.reshape(-1, D)
    input_grad = drows.reshape(-1, D)
    return (block_out, input_grad, totals[0], totals[1], totals[2], totals[3], totals[4], totals[5], totals[6], totals[7], totals[8], totals[9], totals[10], totals[11])
```

```python
import functools

import jax
import jax.numpy as jnp
import numpy as np
from jax import lax
from jax.experimental import pallas as pl
from jax.experimental.pallas import tpu as pltpu
from jax.sharding import PartitionSpec as P

ROT = 16
LEN = 1024
EPSILON = 1e-05
ROTARY_BASE = 10000.0
MASKED = -1e30
VMEM_LIMIT = 56 * 1024 * 1024
BF = jnp.bfloat16
F32 = jnp.float32


def mm(a, b):
    return lax.dot_general(a, b, (((1,), (0,)), ((), ())), preferred_element_type=F32)


def mm_nt(a, b):
    return lax.dot_general(a, b, (((1,), (1,)), ((), ())), preferred_element_type=F32)


def mm_tn(a, b):
    return lax.dot_general(a, b, (((0,), (0,)), ((), ())), preferred_element_type=F32)


def fold(array):
    rows, width = array.shape
    return jnp.sum(array.reshape(rows // 8, 8, width), axis=0)


def standardise(rows):
    width = rows.shape[-1]
    centred = rows - jnp.sum(rows, axis=-1, keepdims=True) * (1.0 / width)
    spread = jnp.sum(centred * centred, axis=-1, keepdims=True) * (1.0 / width)
    scale = lax.rsqrt(spread + EPSILON)
    return centred * scale, scale


def gelu_parts(value):
    away = jnp.abs(value)
    bell = jnp.exp(value * value * -0.5)
    t = 1.0 / (1.0 + away * (0.3275911 * 0.7071067811865476))
    poly = t * (
        0.127414796
        + t * (-0.142248368 + t * (0.7107068705 + t * (-0.7265760135 + t * 0.5307027145)))
    )
    tail = poly * bell
    phi = jnp.where(value >= 0.0, 1.0 - tail, tail)
    return value * phi, phi + value * bell * 0.3989422804014327


def feed_kernel(
    tok, cot, gain, shift, fcw, fcb, prw, ff, e2, dfc, dproj, dgain, dshift, dfcb, dbias
):
    step = pl.program_id(0)
    xhat, _ = standardise(tok[...].astype(F32))
    normed = (xhat * gain[...] + shift[...]).astype(BF)
    hidden = mm(normed, fcw[...]) + fcb[...]
    act, slope = gelu_parts(hidden)
    act = act.astype(BF)
    upstream = cot[...]
    ff[...] = mm(act, prw[...]).astype(BF)
    dhidden = (mm_nt(upstream, prw[...]) * slope).astype(BF)
    dnormed = mm_nt(dhidden, fcw[...])
    e2[...] = (dnormed * gain[...]).astype(BF)

    @pl.when(step == 0)
    def _():
        for ref in (dfc, dproj, dgain, dshift, dfcb, dbias):
            ref[...] = jnp.zeros(ref.shape, F32)

    dproj[...] += mm_tn(act, upstream)
    dfc[...] += mm_tn(normed, dhidden)
    dgain[...] += fold(dnormed * xhat)
    dshift[...] += fold(dnormed)
    dfcb[...] += fold(dhidden.astype(F32))
    dbias[...] += fold(upstream.astype(F32))


def feed(tokens, cotangent, gain, shift, fcw, fcb, prw, first, count, tile):
    rows, width = tokens.shape
    units = fcw.shape[1]
    base = first // tile
    steps = count // tile
    source = pl.BlockSpec((tile, width), lambda i: (i + base, 0))
    target = pl.BlockSpec((tile, width), lambda i: (i, 0))

    def whole(*shape):
        return pl.BlockSpec(shape, lambda i: (0,) * len(shape))

    return pl.pallas_call(
        feed_kernel,
        grid=(steps,),
        in_specs=[
            source,
            source,
            whole(1, width),
            whole(1, width),
            whole(width, units),
            whole(1, units),
            whole(units, width),
        ],
        out_specs=[
            target,
            target,
            whole(width, units),
            whole(units, width),
            whole(8, width),
            whole(8, width),
            whole(8, units),
            whole(8, width),
        ],
        out_shape=[
            jax.ShapeDtypeStruct((count, width), BF),
            jax.ShapeDtypeStruct((count, width), BF),
            jax.ShapeDtypeStruct((width, units), F32),
            jax.ShapeDtypeStruct((units, width), F32),
            jax.ShapeDtypeStruct((8, width), F32),
            jax.ShapeDtypeStruct((8, width), F32),
            jax.ShapeDtypeStruct((8, units), F32),
            jax.ShapeDtypeStruct((8, width), F32),
        ],
        compiler_params=pltpu.CompilerParams(vmem_limit_bytes=VMEM_LIMIT),
        cost_estimate=pl.CostEstimate(
            flops=12 * count * width * units,
            bytes_accessed=8 * count * width + 12 * width * units,
            transcendentals=2 * count * units,
        ),
        name="feed",
    )(tokens, cotangent, gain, shift, fcw, fcb, prw)


def partner(array, lane):
    half = ROT // 2
    width = array.shape[-1]
    return jnp.where(
        lane < half,
        pltpu.roll(array, width - half, 1),
        pltpu.roll(array, half, 1),
    )


def attend_kernel(
    head,
    chunk,
    block,
    core,
    tok,
    cot,
    ff,
    e2,
    gain,
    shift,
    wqkv,
    bqkv,
    wdense,
    cosine,
    sine,
    give,
    keep,
    dqkv,
    ddense,
    dgain,
    dshift,
    dbqkv,
    xhat_s,
    scale_s,
    n1_s,
    q_s,
    k_s,
    v_s,
    dc_s,
    ctx_s,
    dm_s,
    p_s,
    d_s,
    dqk_s,
):
    length, width = tok.shape
    heads = q_s.shape[0]
    triple = 3 * head
    half_rows = length // 2
    lane = lax.broadcasted_iota(jnp.int32, (chunk, 2 * head), 1) % head

    def before(i, carry):
        rows = pl.ds(pl.multiple_of(i * chunk, chunk), chunk)
        xhat, scale = standardise(tok[rows, :].astype(F32))
        xhat_s[rows, :] = xhat
        scale_s[rows, :] = scale
        normed = (xhat * gain[...] + shift[...]).astype(BF)
        n1_s[rows, :] = normed
        cos, sin = cosine[rows, :], sine[rows, :]
        dctx = mm_nt(cot[rows, :], wdense[...]).astype(BF)
        for h in range(heads):
            mixed = mm_nt(normed, wqkv[h * triple : (h + 1) * triple, :]) + bqkv[h : h + 1, :]
            turn = mixed[:, : 2 * head]
            turned = turn * cos + partner(turn, lane) * sin
            q_s[h, rows, :] = (turned[:, :head] * head**-0.5).astype(BF)
            k_s[h, rows, :] = turned[:, head:].astype(BF)
            v_s[h, rows, :] = mixed[:, 2 * head :].astype(BF)
            dc_s[h, rows, :] = dctx[:, h * head : (h + 1) * head]
        return carry

    lax.fori_loop(0, length // chunk, before, 0)

    causal = lax.broadcasted_iota(jnp.int32, (block, block), 1) <= lax.broadcasted_iota(
        jnp.int32, (block, block), 0
    )
    count = length // block

    def one_head(h, carry):
        for i in range(count):
            low, high = i * block, (i + 1) * block
            query = q_s[h, low:high, :]
            dctx = dc_s[h, low:high, :]
            pieces = [(low, high)] if i == 0 else [(0, low), (low, high)]
            scores = []
            for start, stop in pieces:
                part = mm_nt(query, k_s[h, start:stop, :])
                if start == low:
                    part = jnp.where(causal, part, MASKED)
                scores.append(part)
            top = functools.reduce(
                jnp.maximum, [jnp.max(part, axis=-1, keepdims=True) for part in scores]
            )
            scores = [jnp.exp(part - top) for part in scores]
            total = sum(jnp.sum(part, axis=-1, keepdims=True) for part in scores)
            inverse = 1.0 / total
            probs = [part * inverse for part in scores]
            context = 0.0
            for (start, stop), part in zip(pieces, probs):
                rounded = part.astype(BF)
                p_s[low:high, start:stop] = rounded
                context = context + mm(rounded, v_s[h, start:stop, :])
            ctx_s[h, low:high, :] = context.astype(BF)
            inner = jnp.sum(context * dctx.astype(F32), axis=-1, keepdims=True)
            dquery = 0.0
            for (start, stop), part in zip(pieces, probs):
                dprobs = mm_nt(dctx, v_s[h, start:stop, :])
                dscores = (part * (dprobs - inner)).astype(BF)
                d_s[low:high, start:stop] = dscores
                dquery = dquery + mm(dscores, k_s[h, start:stop, :])
            dqk_s[low:high, :head] = dquery * head**-0.5
        for j in range(count):
            low, high = j * block, (j + 1) * block
            dqk_s[low:high, head:] = mm_tn(d_s[low:, low:high], q_s[h, low:, :])
            dvalue = mm_tn(p_s[low:, low:high], dc_s[h, low:, :])
            dm_s[h, low:high, 2 * head :] = dvalue.astype(BF)
        for j in range(length // chunk):
            low, high = j * chunk, (j + 1) * chunk
            turn = dqk_s[low:high, :]
            back = turn * cosine[low:high, :] - partner(turn, lane) * sine[low:high, :]
            dm_s[h, low:high, : 2 * head] = back.astype(BF)
        return carry

    lax.fori_loop(0, heads, one_head, 0)

    for ref in (dgain, dshift, dbqkv):
        ref[...] = jnp.zeros(ref.shape, F32)

    def after(i, carry):
        rows = pl.ds(pl.multiple_of(i * chunk, chunk), chunk)
        context = jnp.concatenate([ctx_s[h, rows, :] for h in range(heads)], axis=-1)
        part = mm(context, wdense[...]) + ff[rows, :].astype(F32)
        dnormed = 0.0
        for h in range(heads):
            dmixed = dm_s[h, rows, :]
            dnormed = dnormed + mm(dmixed, wqkv[h * triple : (h + 1) * triple, :])
            dbqkv[h * 8 : (h + 1) * 8, :] += fold(dmixed.astype(F32))
        xhat, scale = xhat_s[rows, :], scale_s[rows, :]
        dgain[...] += fold(dnormed * xhat)
        dshift[...] += fold(dnormed)
        pulled = dnormed * gain[...] + e2[rows, :].astype(F32)
        mean = jnp.sum(pulled, axis=-1, keepdims=True) * (1.0 / width)
        along = jnp.sum(pulled * xhat, axis=-1, keepdims=True) * (1.0 / width)
        dinput = (scale * (pulled - mean - xhat * along)).astype(BF)
        side = (i * chunk) // half_rows
        there = pl.ds(pl.multiple_of(i * chunk - side * half_rows, chunk), chunk)

        @pl.when(side == core[0])
        def _():
            keep[0, there, :] = part.astype(BF)
            keep[1, there, :] = dinput

        @pl.when(side != core[0])
        def _():
            give[0, there, :] = part.astype(BF)
            give[1, there, :] = dinput

        return carry

    lax.fori_loop(0, length // chunk, after, 0)
    for h in range(heads):
        dqkv[h * triple : (h + 1) * triple, :] = mm_tn(dm_s[h], n1_s[...])
        ddense[h * head : (h + 1) * head, :] = mm_tn(ctx_s[h], cot[...])


def attend(core, tokens, cotangent, ff, e2, gain, shift, wqkv, bqkv, wdense, tables, seq, ff_seq):
    width = tokens.shape[1]
    heads, triple = bqkv.shape
    head = triple // 3
    chunk, block = 256, 256
    half = LEN // 2

    def rows_of(index):
        return pl.BlockSpec((LEN, width), lambda i: (index, 0))

    def whole(*shape):
        return pl.BlockSpec(shape, lambda i: (0,) * len(shape))

    flops = 6 * LEN * width * 4 * heads * head + 12 * heads * LEN * LEN * head
    return pl.pallas_call(
        functools.partial(attend_kernel, head, chunk, block),
        grid=(1,),
        in_specs=[
            pl.BlockSpec(memory_space=pltpu.SMEM),
            rows_of(seq),
            rows_of(seq),
            rows_of(ff_seq),
            rows_of(ff_seq),
            whole(1, width),
            whole(1, width),
            whole(heads * triple, width),
            whole(heads, triple),
            whole(heads * head, width),
            whole(LEN, 2 * head),
            whole(LEN, 2 * head),
        ],
        out_specs=[
            whole(2, half, width),
            whole(2, half, width),
            whole(heads * triple, width),
            whole(heads * head, width),
            whole(8, width),
            whole(8, width),
            whole(8 * heads, triple),
        ],
        out_shape=[
            jax.ShapeDtypeStruct((2, half, width), BF),
            jax.ShapeDtypeStruct((2, half, width), BF),
            jax.ShapeDtypeStruct((heads * triple, width), F32),
            jax.ShapeDtypeStruct((heads * head, width), F32),
            jax.ShapeDtypeStruct((8, width), F32),
            jax.ShapeDtypeStruct((8, width), F32),
            jax.ShapeDtypeStruct((8 * heads, triple), F32),
        ],
        scratch_shapes=[
            pltpu.VMEM((LEN, width), F32),
            pltpu.VMEM((LEN, 1), F32),
            pltpu.VMEM((LEN, width), BF),
            pltpu.VMEM((heads, LEN, head), BF),
            pltpu.VMEM((heads, LEN, head), BF),
            pltpu.VMEM((heads, LEN, head), BF),
            pltpu.VMEM((heads, LEN, head), BF),
            pltpu.VMEM((heads, LEN, head), BF),
            pltpu.VMEM((heads, LEN, triple), BF),
            pltpu.VMEM((LEN, LEN), BF),
            pltpu.VMEM((LEN, LEN), BF),
            pltpu.VMEM((LEN, 2 * head), F32),
        ],
        compiler_params=pltpu.CompilerParams(vmem_limit_bytes=VMEM_LIMIT),
        cost_estimate=pl.CostEstimate(
            flops=flops,
            bytes_accessed=16 * LEN * width + 10 * 4 * heads * head * width,
            transcendentals=heads * LEN * LEN,
        ),
        name="attend",
    )(core, tokens, cotangent, ff, e2, gain, shift, wqkv, bqkv, wdense, *tables)


def rotary_tables(head):
    half = ROT // 2
    position = np.arange(LEN, dtype=np.float32)
    inverse = (ROTARY_BASE ** (-(np.arange(half) * 2.0) / ROT)).astype(np.float32)
    angle = (position[:, None] * inverse[None, :]).astype(np.float64)
    cosine = np.ones((LEN, head), np.float32)
    sine = np.zeros((LEN, head), np.float32)
    cosine[:, :half] = cosine[:, half:ROT] = np.cos(angle)
    sine[:, :half] = -np.sin(angle)
    sine[:, half:ROT] = np.sin(angle)
    return np.tile(cosine, (1, 2)), np.tile(sine, (1, 2))


def swap(array, axis, bit):
    size = lax.axis_size(axis)
    return lax.ppermute(array, axis, [(i, i ^ bit) for i in range(size)])


def bits_of(size):
    return [1 << b for b in range(size.bit_length() - 1)]


def sum_halving(array, axis, bits):
    index = lax.axis_index(axis)
    for bit in bits:
        half = array.shape[0] // 2
        side = ((index & bit) != 0).astype(jnp.int32)
        sent = lax.dynamic_slice_in_dim(array, (1 - side) * half, half, 0).astype(BF)
        kept = lax.dynamic_slice_in_dim(array, side * half, half, 0)
        array = kept + swap(sent, axis, bit).astype(F32)
    array = array.astype(BF)
    for bit in reversed(bits):
        other = swap(array, axis, bit)
        upper = (index & bit) != 0
        array = jnp.concatenate(
            [jnp.where(upper, other, array), jnp.where(upper, array, other)], axis=0
        )
    return array.astype(F32)


def sum_doubling(array, axis):
    for bit in bits_of(lax.axis_size(axis)):
        array = array + swap(array, axis, bit)
    return array


def local(
    tokens,
    ln1_gain,
    ln1_bias,
    ln2_gain,
    ln2_bias,
    qkv_weight,
    qkv_bias,
    dense_weight,
    dense_bias,
    fc_weight,
    fc_bias,
    proj_weight,
    proj_bias,
    cotangent,
):
    rows, width = tokens.shape
    heads, triple = qkv_bias.shape
    units = fc_weight.shape[1]
    seqs = rows // LEN
    half = LEN // 2
    place = lax.axis_index("tensor")
    core = place % 2
    dp_bits = bits_of(lax.axis_size("dp"))
    wqkv = qkv_weight.transpose(1, 2, 0).reshape(heads * triple, width)
    bqkv = qkv_bias.astype(F32)
    tables = rotary_tables(triple // 3)
    row = lambda vector: vector.astype(F32).reshape(1, -1)

    ff, e2, dfc, dproj, dgain2, dshift2, dfcb, dbias = feed(
        tokens,
        cotangent,
        row(ln2_gain),
        row(ln2_bias),
        fc_weight,
        row(fc_bias),
        proj_weight,
        0,
        rows,
        512,
    )
    dproj = sum_halving(dproj, "dp", dp_bits)
    dfc = sum_halving(dfc, "dp", dp_bits[1:] + dp_bits[:1])

    out_base = dense_bias.astype(F32) + proj_bias.astype(F32)
    block_out = jnp.zeros((rows, width), BF)
    input_grad = jnp.zeros((rows, width), F32)
    grads = []
    for s in range(seqs):
        give, keep, *more = attend(
            core.reshape(1).astype(jnp.int32),
            tokens,
            cotangent,
            ff,
            e2,
            row(ln1_gain),
            row(ln1_bias),
            wqkv,
            bqkv,
            dense_weight,
            tables,
            s,
            s,
        )
        grads.append(more)
        mine = (keep.astype(F32) + swap(give, "tensor", 1).astype(F32)).astype(BF)
        whole = mine.astype(F32) + swap(mine, "tensor", 2).astype(F32)
        start = s * LEN + core * half
        other = s * LEN + (1 - core) * half
        here = lax.dynamic_slice_in_dim(tokens, start, half, 0).astype(F32)
        out_half = (here + whole[0] + out_base).astype(BF)
        grad_half = lax.dynamic_slice_in_dim(cotangent, start, half, 0).astype(F32) + whole[1]
        block_out = lax.dynamic_update_slice_in_dim(block_out, out_half, start, 0)
        input_grad = lax.dynamic_update_slice_in_dim(input_grad, grad_half, start, 0)
        block_out = lax.dynamic_update_slice_in_dim(
            block_out, swap(out_half, "tensor", 1), other, 0
        )
        input_grad = lax.dynamic_update_slice_in_dim(
            input_grad, swap(grad_half, "tensor", 1), other, 0
        )
    dqkv, ddense, dgain1, dshift1, dbqkv = [sum(parts) for parts in zip(*grads)]
    packed = sum_halving(jnp.concatenate([dqkv, ddense], axis=0), "dp", dp_bits)
    dqkv = packed[: heads * triple].reshape(heads, triple, width).transpose(2, 0, 1)
    ddense = packed[heads * triple :]

    dbqkv = dbqkv.reshape(heads, 8, triple).sum(axis=1).reshape(-1)
    vectors = [dgain1.sum(0), dshift1.sum(0), dgain2.sum(0), dshift2.sum(0)]
    vectors += [dfcb.sum(0), dbias.sum(0), dbqkv]
    sizes = [vector.shape[0] for vector in vectors]
    total = sum(sizes)
    lanes = 1024
    flat = jnp.concatenate(vectors + [jnp.zeros((-total % lanes,), F32)]).reshape(-1, lanes)
    flat = sum_doubling(flat, "dp")
    norms = sum_doubling(flat.reshape(-1)[: 4 * width].reshape(4, width), "tensor")
    flat = flat.reshape(-1)
    offsets = np.cumsum([0] + sizes)
    dfcb, dbias, dbqkv = [flat[offsets[i] : offsets[i + 1]] for i in (4, 5, 6)]
    return (
        block_out,
        input_grad,
        norms[0],
        norms[1],
        norms[2],
        norms[3],
        dqkv,
        dbqkv.reshape(heads, triple),
        ddense,
        dbias,
        dfc,
        dfcb,
        dproj,
        dbias,
    )


def solution(mesh):
    in_specs = (
        P("dp", None),
        P(),
        P(),
        P(),
        P(),
        P(None, "tensor", None),
        P("tensor", None),
        P("tensor", None),
        P(),
        P(None, "tensor"),
        P("tensor"),
        P("tensor", None),
        P(),
        P("dp", None),
    )
    out_specs = (
        P("dp", None),
        P("dp", None),
        P(),
        P(),
        P(),
        P(),
        P(None, "tensor", None),
        P("tensor", None),
        P("tensor", None),
        P(),
        P(None, "tensor"),
        P("tensor"),
        P("tensor", None),
        P(),
    )
    return jax.shard_map(local, mesh=mesh, in_specs=in_specs, out_specs=out_specs, check_vma=False)
```

```python
import functools

import jax
import jax.numpy as jnp
import numpy as np
from jax import lax
from jax.experimental import pallas as pl
from jax.experimental.pallas import tpu as pltpu
from jax.sharding import PartitionSpec as P

ROT = 16
LEN = 1024
EPSILON = 1e-05
ROTARY_BASE = 10000.0
MASKED = -1e30
VMEM_LIMIT = 56 * 1024 * 1024
BF = jnp.bfloat16
F32 = jnp.float32


def mm(a, b):
    return lax.dot_general(a, b, (((1,), (0,)), ((), ())), preferred_element_type=F32)


def mm_nt(a, b):
    return lax.dot_general(a, b, (((1,), (1,)), ((), ())), preferred_element_type=F32)


def mm_tn(a, b):
    return lax.dot_general(a, b, (((0,), (0,)), ((), ())), preferred_element_type=F32)


def fold(array):
    rows, width = array.shape
    return jnp.sum(array.reshape(rows // 8, 8, width), axis=0)


def standardise(rows):
    width = rows.shape[-1]
    centred = rows - jnp.sum(rows, axis=-1, keepdims=True) * (1.0 / width)
    spread = jnp.sum(centred * centred, axis=-1, keepdims=True) * (1.0 / width)
    scale = lax.rsqrt(spread + EPSILON)
    return centred * scale, scale


def gelu_parts(value):
    phi = 0.5 + 0.5 * lax.erf(value * 0.7071067811865476)
    bell = jnp.exp(value * value * -0.5)
    return value * phi, phi + value * bell * 0.3989422804014327


def feed_kernel(core, tok, cot, gain, shift, fcw, fcb, prw, *rest):
    ff, e2, dweights, dgain, dshift, dfcb, dbias, stamp, _, _ = rest[-10:]
    units = fcw.shape[1]
    step = pl.program_id(0)
    stamp[0] = core[0]
    xhat, _ = standardise(tok[...].astype(F32))
    normed = (xhat * gain[...] + shift[...]).astype(BF)
    hidden = mm(normed, fcw[...]) + fcb[...]
    act, slope = gelu_parts(hidden)
    act = act.astype(BF)
    upstream = cot[...]
    ff[...] = mm(act, prw[...]).astype(BF)
    dhidden = (mm_nt(upstream, prw[...]) * slope).astype(BF)
    dnormed = mm_nt(dhidden, fcw[...])
    e2[...] = (dnormed * gain[...]).astype(BF)

    @pl.when(step == 0)
    def _():
        for ref in (dweights, dgain, dshift, dfcb, dbias):
            ref[...] = jnp.zeros(ref.shape, F32)

    dweights[:units, :] += mm_tn(act, upstream)
    dweights[units:, :] += mm_tn(normed, dhidden)
    dgain[...] += fold(dnormed * xhat)
    dshift[...] += fold(dnormed)
    dfcb[...] += fold(dhidden.astype(F32))
    dbias[...] += fold(upstream.astype(F32))


def feed(core, tokens, cotangent, gain, shift, fcw, fcb, prw, first, count, tile, after=()):
    rows, width = tokens.shape
    units = fcw.shape[1]
    base = first // tile
    steps = count // tile
    source = pl.BlockSpec((tile, width), lambda i: (i + base, 0))
    target = pl.BlockSpec((tile, width), lambda i: (i, 0))

    def whole(*shape):
        return pl.BlockSpec(shape, lambda i: (0,) * len(shape))

    return pl.pallas_call(
        feed_kernel,
        grid=(steps,),
        in_specs=[
            pl.BlockSpec(memory_space=pltpu.SMEM),
            source,
            source,
            whole(1, width),
            whole(1, width),
            whole(width, units),
            whole(1, units),
            whole(units, width),
        ]
        + [pl.BlockSpec(memory_space=pl.ANY)] * len(after),
        out_specs=[
            target,
            target,
            whole(units + width, width),
            whole(8, width),
            whole(8, width),
            whole(8, units),
            whole(8, width),
            pl.BlockSpec(memory_space=pltpu.SMEM),
            pl.BlockSpec(memory_space=pl.ANY),
            pl.BlockSpec(memory_space=pl.ANY),
        ],
        out_shape=[
            jax.ShapeDtypeStruct((count, width), BF),
            jax.ShapeDtypeStruct((count, width), BF),
            jax.ShapeDtypeStruct((units + width, width), F32),
            jax.ShapeDtypeStruct((8, width), F32),
            jax.ShapeDtypeStruct((8, width), F32),
            jax.ShapeDtypeStruct((8, units), F32),
            jax.ShapeDtypeStruct((8, width), F32),
            jax.ShapeDtypeStruct((1,), jnp.int32),
            jax.ShapeDtypeStruct((rows, width), BF),
            jax.ShapeDtypeStruct((rows, width), F32),
        ],
        compiler_params=pltpu.CompilerParams(vmem_limit_bytes=VMEM_LIMIT),
        cost_estimate=pl.CostEstimate(flops=1, bytes_accessed=1, transcendentals=0),
        name="feed",
    )(core, tokens, cotangent, gain, shift, fcw, fcb, prw, *after)


def gate_kernel(passed, core, *refs):
    refs[-1][0] = core[0]


def gate(core, ready, passed):
    anywhere = pl.BlockSpec(memory_space=pl.ANY)
    scalar = pl.BlockSpec(memory_space=pltpu.SMEM)
    *handed, stamp = pl.pallas_call(
        functools.partial(gate_kernel, len(passed)),
        in_specs=[scalar] + [anywhere] * (len(passed) + len(ready)),
        out_specs=[anywhere] * len(passed) + [scalar],
        out_shape=[jax.ShapeDtypeStruct(a.shape, a.dtype) for a in passed]
        + [jax.ShapeDtypeStruct((1,), jnp.int32)],
        input_output_aliases={1 + k: k for k in range(len(passed))},
        cost_estimate=pl.CostEstimate(flops=1, bytes_accessed=1, transcendentals=0),
        name="gate",
    )(core, *passed, *ready)
    return handed, stamp[0]


def settle_kernel(parts, core, mine, other, *refs):
    bases, (shift,) = refs[:parts], refs[parts : parts + 1]
    halves, outs = refs[-2 * parts : -parts], refs[-parts:]
    for k in range(parts):
        total = mine[k].astype(F32) + other[k].astype(F32) + bases[k][...].astype(F32) + shift[k]
        total = total.astype(halves[k].dtype)
        halves[k][...] = total
        outs[k][...] = total


def settle(core, seq, mine, other, bases, shift, outs, after):
    parts, half, width = mine.shape
    chunk = half // 2
    stacked = pl.BlockSpec((parts, chunk, width), lambda i, core: (0, i, 0))
    rows = pl.BlockSpec((chunk, width), lambda i, core: ((seq * 2 + core[0]) * 2 + i, 0))
    anywhere = pl.BlockSpec(memory_space=pl.ANY)
    fixed = 1 + 2 + parts + 1
    return pl.pallas_call(
        functools.partial(settle_kernel, parts),
        grid_spec=pltpu.PrefetchScalarGridSpec(
            num_scalar_prefetch=1,
            grid=(2,),
            in_specs=[stacked, stacked]
            + [rows] * parts
            + [pl.BlockSpec((parts, 1, width), lambda i, core: (0, 0, 0))]
            + [anywhere] * (parts + len(after)),
            out_specs=[pl.BlockSpec((chunk, width), lambda i, core: (i, 0))] * parts
            + [rows] * parts,
        ),
        out_shape=[jax.ShapeDtypeStruct((half, width), a.dtype) for a in outs]
        + [jax.ShapeDtypeStruct(a.shape, a.dtype) for a in outs],
        input_output_aliases={fixed + k: parts + k for k in range(parts)},
        cost_estimate=pl.CostEstimate(flops=1, bytes_accessed=1, transcendentals=0),
        name="settle",
    )(core, mine, other, *bases, shift, *outs, *after)


def place_kernel(parts, core, *refs):
    for k in range(parts):
        refs[2 * parts + k][...] = refs[k][...]


def place(core, seq, halves, outs):
    parts = len(halves)
    half, width = halves[0].shape
    chunk = half // 2
    return pl.pallas_call(
        functools.partial(place_kernel, parts),
        grid_spec=pltpu.PrefetchScalarGridSpec(
            num_scalar_prefetch=1,
            grid=(2,),
            in_specs=[pl.BlockSpec((chunk, width), lambda i, core: (i, 0))] * parts
            + [pl.BlockSpec(memory_space=pl.ANY)] * parts,
            out_specs=[
                pl.BlockSpec(
                    (chunk, width), lambda i, core: ((seq * 2 + 1 - core[0]) * 2 + i, 0)
                )
            ]
            * parts,
        ),
        out_shape=[jax.ShapeDtypeStruct(a.shape, a.dtype) for a in outs],
        input_output_aliases={1 + parts + k: k for k in range(parts)},
        cost_estimate=pl.CostEstimate(flops=1, bytes_accessed=1, transcendentals=0),
        name="place",
    )(core, *halves, *outs)


def partner(array, lane):
    half = ROT // 2
    width = array.shape[-1]
    return jnp.where(
        lane < half,
        pltpu.roll(array, width - half, 1),
        pltpu.roll(array, half, 1),
    )


def attend_kernel(head, chunk, block, more, waits, core, *refs):
    tok, cot, ff, e2, gain, shift, wqkv, bqkv, wdense, cosine, sine = refs[:11]
    carried = refs[11 : 11 + 4 * more]
    waits += 4 * more
    *give, keep, dweights, dgain, dshift, dbqkv, stamp = refs[11 + waits : 21 + waits]
    xhat_s, scale_s, n1_s, q_s, k_s, v_s, dc_s, ctx_s, dm_s, p_s, d_s, dqk_s = refs[21 + waits :]
    stamp[0] = core[0]
    length, width = tok.shape
    heads = q_s.shape[0]
    triple = 3 * head
    half_rows = length // 2
    lane = lax.broadcasted_iota(jnp.int32, (chunk, 2 * head), 1) % head

    def before(i, carry):
        rows = pl.ds(pl.multiple_of(i * chunk, chunk), chunk)
        xhat, scale = standardise(tok[rows, :].astype(F32))
        xhat_s[rows, :] = xhat
        scale_s[rows, :] = scale
        normed = (xhat * gain[...] + shift[...]).astype(BF)
        n1_s[rows, :] = normed
        cos, sin = cosine[rows, :], sine[rows, :]
        dctx = mm_nt(cot[rows, :], wdense[...]).astype(BF)
        for h in range(heads):
            mixed = mm_nt(normed, wqkv[h * triple : (h + 1) * triple, :]) + bqkv[h : h + 1, :]
            turn = mixed[:, : 2 * head]
            turned = turn * cos + partner(turn, lane) * sin
            q_s[h, rows, :] = (turned[:, :head] * head**-0.5).astype(BF)
            k_s[h, rows, :] = turned[:, head:].astype(BF)
            v_s[h, rows, :] = mixed[:, 2 * head :].astype(BF)
            dc_s[h, rows, :] = dctx[:, h * head : (h + 1) * head]
        return carry

    lax.fori_loop(0, length // chunk, before, 0)

    causal = lax.broadcasted_iota(jnp.int32, (block, block), 1) <= lax.broadcasted_iota(
        jnp.int32, (block, block), 0
    )
    count = length // block

    def one_head(h, carry):
        for i in range(count):
            low, high = i * block, (i + 1) * block
            query = q_s[h, low:high, :]
            dctx = dc_s[h, low:high, :]
            pieces = [(low, high)] if i == 0 else [(0, low), (low, high)]
            scores = []
            for start, stop in pieces:
                part = mm_nt(query, k_s[h, start:stop, :])
                if start == low:
                    part = jnp.where(causal, part, MASKED)
                scores.append(part)
            top = functools.reduce(
                jnp.maximum, [jnp.max(part, axis=-1, keepdims=True) for part in scores]
            )
            scores = [jnp.exp(part - top) for part in scores]
            total = sum(jnp.sum(part, axis=-1, keepdims=True) for part in scores)
            inverse = 1.0 / total
            probs = [part * inverse for part in scores]
            context = 0.0
            for (start, stop), part in zip(pieces, probs):
                rounded = part.astype(BF)
                p_s[low:high, start:stop] = rounded
                context = context + mm(rounded, v_s[h, start:stop, :])
            ctx_s[h, low:high, :] = context.astype(BF)
            inner = jnp.sum(context * dctx.astype(F32), axis=-1, keepdims=True)
            dquery = 0.0
            for (start, stop), part in zip(pieces, probs):
                dprobs = mm_nt(dctx, v_s[h, start:stop, :])
                dscores = (part * (dprobs - inner)).astype(BF)
                d_s[low:high, start:stop] = dscores
                dquery = dquery + mm(dscores, k_s[h, start:stop, :])
            dqk_s[low:high, :head] = dquery * head**-0.5
        for j in range(count):
            low, high = j * block, (j + 1) * block
            dqk_s[low:high, head:] = mm_tn(q_s[h, low:, :], d_s[low:, low:high]).T
            dvalue = mm_tn(dc_s[h, low:, :], p_s[low:, low:high]).T
            dm_s[h, low:high, 2 * head :] = dvalue.astype(BF)
        for j in range(length // chunk):
            low, high = j * chunk, (j + 1) * chunk
            turn = dqk_s[low:high, :]
            back = turn * cosine[low:high, :] - partner(turn, lane) * sine[low:high, :]
            dm_s[h, low:high, : 2 * head] = back.astype(BF)
        return carry

    lax.fori_loop(0, heads, one_head, 0)

    for k, ref in enumerate((dgain, dshift, dbqkv)):
        ref[...] = carried[1 + k][...] if more else jnp.zeros(ref.shape, F32)

    def after(i, carry):
        rows = pl.ds(pl.multiple_of(i * chunk, chunk), chunk)
        context = jnp.concatenate([ctx_s[h, rows, :] for h in range(heads)], axis=-1)
        part = mm(context, wdense[...]) + ff[rows, :].astype(F32)
        dnormed = 0.0
        for h in range(heads):
            dmixed = dm_s[h, rows, :]
            dnormed = dnormed + mm(dmixed, wqkv[h * triple : (h + 1) * triple, :])
            dbqkv[h * 8 : (h + 1) * 8, :] += fold(dmixed.astype(F32))
        xhat, scale = xhat_s[rows, :], scale_s[rows, :]
        dgain[...] += fold(dnormed * xhat)
        dshift[...] += fold(dnormed)
        pulled = dnormed * gain[...] + e2[rows, :].astype(F32)
        mean = jnp.sum(pulled, axis=-1, keepdims=True) * (1.0 / width)
        along = jnp.sum(pulled * xhat, axis=-1, keepdims=True) * (1.0 / width)
        dinput = (scale * (pulled - mean - xhat * along)).astype(BF)
        side = (i * chunk) // half_rows
        there = pl.ds(pl.multiple_of(i * chunk - side * half_rows, chunk), chunk)

        @pl.when(side == core[0])
        def _():
            keep[0, there, :] = part.astype(BF)
            keep[1, there, :] = dinput

        for j in range(2):

            @pl.when((side != core[0]) & (i * chunk == side * half_rows + j * chunk))
            def _():
                give[j][...] = part.astype(BF)
                give[2 + j][...] = dinput

        return carry

    lax.fori_loop(0, length // chunk, after, 0)
    for h in range(heads):
        rows = slice(h * triple, (h + 1) * triple)
        part = mm_tn(dm_s[h], n1_s[...])
        dweights[rows, :] = part + carried[0][rows, :] if more else part
        rows = slice(heads * triple + h * head, heads * triple + (h + 1) * head)
        part = mm_tn(ctx_s[h], cot[...])
        dweights[rows, :] = part + carried[0][rows, :] if more else part


def attend(
    core, tokens, cotangent, ff, e2, gain, shift, wqkv, bqkv, wdense, tables, seq, carried, after
):
    width = tokens.shape[1]
    heads, triple = bqkv.shape
    head = triple // 3
    chunk, block = 256, 512
    half = LEN // 2

    def rows_of(index):
        return pl.BlockSpec((LEN, width), lambda i: (index, 0))

    def whole(*shape):
        return pl.BlockSpec(shape, lambda i: (0,) * len(shape))

    sums = [
        whole(4 * heads * head, width),
        whole(8, width),
        whole(8, width),
        whole(8 * heads, triple),
    ]
    return pl.pallas_call(
        functools.partial(attend_kernel, head, chunk, block, bool(carried), len(after)),
        grid=(1,),
        in_specs=[
            pl.BlockSpec(memory_space=pltpu.SMEM),
            rows_of(seq),
            rows_of(seq),
            rows_of(seq),
            rows_of(seq),
            whole(1, width),
            whole(1, width),
            whole(heads * triple, width),
            whole(heads, triple),
            whole(heads * head, width),
            whole(LEN, 2 * head),
            whole(LEN, 2 * head),
        ]
        + (sums if carried else [])
        + [pl.BlockSpec(memory_space=pl.ANY)] * len(after),
        out_specs=[
            *[whole(half // 2, width)] * 4,
            whole(2, half, width),
            *sums,
            pl.BlockSpec(memory_space=pltpu.SMEM),
        ],
        out_shape=[
            *[jax.ShapeDtypeStruct((half // 2, width), BF)] * 4,
            jax.ShapeDtypeStruct((2, half, width), BF),
            jax.ShapeDtypeStruct((4 * heads * head, width), F32),
            jax.ShapeDtypeStruct((8, width), F32),
            jax.ShapeDtypeStruct((8, width), F32),
            jax.ShapeDtypeStruct((8 * heads, triple), F32),
            jax.ShapeDtypeStruct((1,), jnp.int32),
        ],
        scratch_shapes=[
            pltpu.VMEM((LEN, width), F32),
            pltpu.VMEM((LEN, 1), F32),
            pltpu.VMEM((LEN, width), BF),
            pltpu.VMEM((heads, LEN, head), BF),
            pltpu.VMEM((heads, LEN, head), BF),
            pltpu.VMEM((heads, LEN, head), BF),
            pltpu.VMEM((heads, LEN, head), BF),
            pltpu.VMEM((heads, LEN, head), BF),
            pltpu.VMEM((heads, LEN, triple), BF),
            pltpu.VMEM((LEN, LEN), BF),
            pltpu.VMEM((LEN, LEN), BF),
            pltpu.VMEM((LEN, 2 * head), F32),
        ],
        compiler_params=pltpu.CompilerParams(vmem_limit_bytes=VMEM_LIMIT),
        cost_estimate=pl.CostEstimate(flops=1, bytes_accessed=1, transcendentals=0),
        name="attend",
    )(core, tokens, cotangent, ff, e2, gain, shift, wqkv, bqkv, wdense, *tables, *carried, *after)


def rotary_tables(head):
    half = ROT // 2
    position = np.arange(LEN, dtype=np.float32)
    inverse = (ROTARY_BASE ** (-(np.arange(half) * 2.0) / ROT)).astype(np.float32)
    angle = (position[:, None] * inverse[None, :]).astype(np.float64)
    cosine = np.ones((LEN, head), np.float32)
    sine = np.zeros((LEN, head), np.float32)
    cosine[:, :half] = cosine[:, half:ROT] = np.cos(angle)
    sine[:, :half] = -np.sin(angle)
    sine[:, half:ROT] = np.sin(angle)
    return np.tile(cosine, (1, 2)), np.tile(sine, (1, 2))


def swap(array, axis, bit):
    size = lax.axis_size(axis)
    return lax.ppermute(array, axis, [(i, i ^ bit) for i in range(size)])


def bits_of(size):
    return [1 << b for b in range(size.bit_length() - 1)]


def span(bits):
    masks = [0]
    for bit in bits:
        masks += [mask | bit for mask in masks]
    return masks


class Sum:
    def __init__(self, array, axis, groups, late):
        self.axis = axis
        self.stages = [(bits, True) for bits in groups]
        self.stages += [(bits, False) for bits in reversed(groups)]
        self.array = array
        self.prepare(late)

    def place(self, bits, late):
        index = lax.axis_index(self.axis) + late
        return sum((((index & bit) != 0).astype(jnp.int32) << k) for k, bit in enumerate(bits))

    def prepare(self, late):
        if not self.stages:
            return
        bits, down = self.stages[0]
        if down:
            size = self.array.shape[0] >> len(bits)
            here = self.place(bits, late)
            self.sent = [
                lax.dynamic_slice_in_dim(self.array, (here ^ k) * size, size, 0).astype(BF)
                for k in range(1, 1 << len(bits))
            ]
        else:
            self.sent = [self.array.astype(BF)]

    def step(self, late):
        bits, down = self.stages.pop(0)
        masks = span(bits)
        here = self.place(bits, late)
        if down:
            size = self.array.shape[0] >> len(bits)
            total = lax.dynamic_slice_in_dim(self.array, here * size, size, 0)
            for mask, sent in zip(masks[1:], self.sent):
                total = total + swap(sent, self.axis, mask).astype(F32)
            self.array = total
        else:
            own = self.sent[0]
            parts = [own] + [swap(own, self.axis, mask) for mask in masks[1:]]
            pieces = []
            for k in range(len(parts)):
                piece = parts[k]
                for other in range(1, len(parts)):
                    piece = jnp.where(here == other, parts[k ^ other], piece)
                pieces.append(piece)
            self.array = jnp.concatenate(pieces, axis=0)
        self.prepare(late)

    def finish(self, late):
        while self.stages:
            self.step(late)
        return self.array.astype(F32)


def sum_doubling(array, axis):
    for bit in bits_of(lax.axis_size(axis)):
        array = array + swap(array, axis, bit)
    return array


def local(
    tokens,
    ln1_gain,
    ln1_bias,
    ln2_gain,
    ln2_bias,
    qkv_weight,
    qkv_bias,
    dense_weight,
    dense_bias,
    fc_weight,
    fc_bias,
    proj_weight,
    proj_bias,
    cotangent,
):
    rows, width = tokens.shape
    heads, triple = qkv_bias.shape
    units = fc_weight.shape[1]
    seqs = rows // LEN
    half = LEN // 2
    core = lax.axis_index("tensor") % 2
    dp_bits = bits_of(lax.axis_size("dp"))
    wqkv = qkv_weight.transpose(1, 2, 0).reshape(heads * triple, width)
    bqkv = qkv_bias.astype(F32)
    tables = rotary_tables(triple // 3)
    row = lambda vector: vector.astype(F32).reshape(1, -1)

    core_ref = core.reshape(1).astype(jnp.int32)

    def attend_rows(s, carried, after):
        *give, keep, a, b, c, d, stamp = attend(
            core_ref,
            tokens,
            cotangent,
            ff,
            e2,
            row(ln1_gain),
            row(ln1_bias),
            wqkv,
            bqkv,
            dense_weight,
            tables,
            s,
            carried,
            after,
        )
        return give, keep, (a, b, c, d), stamp[0]

    def cross(give, keep):
        others = [swap(piece, "tensor", 1) for piece in give]
        return [
            (keep[k].astype(F32) + jnp.concatenate(others[2 * k : 2 * k + 2]).astype(F32)).astype(BF)
            for k in range(2)
        ]

    shift = jnp.stack(
        [dense_bias.astype(F32) + proj_bias.astype(F32), jnp.zeros((width,), F32)]
    ).reshape(2, 1, width)
    bases = [tokens, cotangent]

    groups = [(dp_bits[0],), tuple(dp_bits[1:3])] + [(bit,) for bit in dp_bits[3:]]
    ff, e2, dfeed, dgain2, dshift2, dfcb, dbias, stamp, *outs = feed(
        core_ref,
        tokens,
        cotangent,
        row(ln2_gain),
        row(ln2_bias),
        fc_weight,
        row(fc_bias),
        proj_weight,
        0,
        rows,
        512,
    )
    now = stamp[0]
    work = Sum(dfeed, "dp", groups, now - core)
    mine, settled, carried = [], [], ()
    after = tuple(work.sent)
    for s in range(seqs):
        give, keep, carried, now = attend_rows(s, carried, after)
        work.step(now - core)
        give, _ = gate(core_ref, work.sent, give)
        if s >= 1:
            other = swap(mine[s - 1], "tensor", 2)
            (keep,), now = gate(core_ref, [other], [keep])
        mine.append(cross(give, keep))
        after = (*mine[s], *work.sent)
        if s < seqs - 1:
            mine[s] = jnp.stack(mine[s])
            after = (mine[s], *work.sent)
        if s >= 1:
            last = mine[s - 1]
            *halves, outs[0], outs[1] = settle(
                core_ref, s - 1, last, other, bases, shift, outs, after
            )
            settled.append(halves)
            after += tuple(halves)

    dgain1, dshift1, dbqkv = carried[1:]
    dbqkv = dbqkv.reshape(heads, 8, triple).sum(axis=1).reshape(-1)
    vectors = [dgain1.sum(0), dshift1.sum(0), dgain2.sum(0), dshift2.sum(0)]
    vectors += [dfcb.sum(0), dbias.sum(0), dbqkv]
    sizes = [vector.shape[0] for vector in vectors]
    total = sum(sizes)
    lanes = 1024
    flat = jnp.concatenate(vectors + [jnp.zeros((-total % lanes,), F32)]).reshape(-1, lanes)
    packed = Sum(carried[0], "dp", groups, now - core)
    handed, stamp = gate(core_ref, [other], [packed.sent[0]])
    packed.sent[:1] = handed
    packed.step(stamp - core)
    halves = []
    for s, parts in enumerate(settled):
        outs = list(place(core_ref, s, [swap(part, "tensor", 1) for part in parts], outs))
    for k in range(2):
        last = mine[-1][k][None]
        part, outs[k] = settle(
            core_ref,
            seqs - 1,
            last,
            swap(last, "tensor", 2),
            bases[k : k + 1],
            shift[k : k + 1],
            outs[k : k + 1],
            (),
        )
        halves.append(part)
        if k == 0:
            (flat,), stamp = gate(core_ref, [part], [flat])
        if packed.stages:
            packed.step(stamp - core)
            (packed.sent[0],), stamp = gate(core_ref, [part], [packed.sent[0]])
    outs = place(core_ref, seqs - 1, [swap(part, "tensor", 1) for part in halves], outs)
    block_out, input_grad = outs
    flat = sum_doubling(flat, "dp")
    norms = sum_doubling(flat.reshape(-1)[: 4 * width].reshape(4, width), "tensor")
    flat = flat.reshape(-1)
    now = stamp
    packed = packed.finish(now - core)
    both = work.finish(now - core)
    dproj, dfc = both[:units], both[units:]
    dqkv = packed[: heads * triple].reshape(heads, triple, width).transpose(2, 0, 1)
    ddense = packed[heads * triple :]

    offsets = np.cumsum([0] + sizes)
    dfcb, dbias, dbqkv = [flat[offsets[i] : offsets[i + 1]] for i in (4, 5, 6)]
    return (
        block_out,
        input_grad,
        norms[0],
        norms[1],
        norms[2],
        norms[3],
        dqkv,
        dbqkv.reshape(heads, triple),
        ddense,
        dbias,
        dfc,
        dfcb,
        dproj,
        dbias,
    )


def solution(mesh):
    in_specs = (
        P("dp", None),
        P(),
        P(),
        P(),
        P(),
        P(None, "tensor", None),
        P("tensor", None),
        P("tensor", None),
        P(),
        P(None, "tensor"),
        P("tensor"),
        P("tensor", None),
        P(),
        P("dp", None),
    )
    out_specs = (
        P("dp", None),
        P("dp", None),
        P(),
        P(),
        P(),
        P(),
        P(None, "tensor", None),
        P("tensor", None),
        P("tensor", None),
        P(),
        P(None, "tensor"),
        P("tensor"),
        P("tensor", None),
        P(),
    )
    return jax.shard_map(local, mesh=mesh, in_specs=in_specs, out_specs=out_specs, check_vma=False)
```

```python
import functools

import jax
import jax.numpy as jnp
import numpy as np
from jax import lax
from jax.experimental import pallas as pl
from jax.experimental.pallas import tpu as pltpu
from jax.sharding import PartitionSpec as P

ROT = 16
LEN = 1024
EPSILON = 1e-05
ROTARY_BASE = 10000.0
MASKED = -1e30
VMEM_LIMIT = 56 * 1024 * 1024
BF = jnp.bfloat16
F32 = jnp.float32


def mm(a, b):
    return lax.dot_general(a, b, (((1,), (0,)), ((), ())), preferred_element_type=F32)


def mm_nt(a, b):
    return lax.dot_general(a, b, (((1,), (1,)), ((), ())), preferred_element_type=F32)


def mm_tn(a, b):
    return lax.dot_general(a, b, (((0,), (0,)), ((), ())), preferred_element_type=F32)


def fold(array):
    rows, width = array.shape
    return jnp.sum(array.reshape(rows // 8, 8, width), axis=0)


def standardise(rows):
    width = rows.shape[-1]
    centred = rows - jnp.sum(rows, axis=-1, keepdims=True) * (1.0 / width)
    spread = jnp.sum(centred * centred, axis=-1, keepdims=True) * (1.0 / width)
    scale = lax.rsqrt(spread + EPSILON)
    return centred * scale, scale


def gelu_parts(value):
    phi = 0.5 + 0.5 * lax.erf(value * 0.7071067811865476)
    bell = jnp.exp(value * value * -0.5)
    return value * phi, phi + value * bell * 0.3989422804014327


def feed_kernel(core, tok, cot, vectors, fcw, prw, *rest):
    ff, e2, dweights, dgain, dshift, dfcb, dbias, stamp, _, _ = rest[-10:]
    width, units = fcw.shape
    gain, shift = vectors[:, :width], vectors[:, width : 2 * width]
    step = pl.program_id(0)
    stamp[0] = core[0]
    xhat, _ = standardise(tok[...].astype(F32))
    normed = (xhat * gain + shift).astype(BF)
    hidden = mm(normed, fcw[...]) + vectors[:, 2 * width :]
    act, slope = gelu_parts(hidden)
    act = act.astype(BF)
    upstream = cot[...]
    ff[...] = mm(act, prw[...]).astype(BF)
    dhidden = (mm_nt(upstream, prw[...]) * slope).astype(BF)
    dnormed = mm_nt(dhidden, fcw[...])
    e2[...] = (dnormed * gain).astype(BF)

    @pl.when(step == 0)
    def _():
        for ref in (dweights, dgain, dshift, dfcb, dbias):
            ref[...] = jnp.zeros(ref.shape, F32)

    dweights[:units, :] += mm_tn(act, upstream)
    dweights[units:, :] += mm_tn(normed, dhidden)
    dgain[...] += fold(dnormed * xhat)
    dshift[...] += fold(dnormed)
    dfcb[...] += fold(dhidden.astype(F32))
    dbias[...] += fold(upstream.astype(F32))


def feed(core, tokens, cotangent, vectors, fcw, prw, first, count, tile, after=()):
    rows, width = tokens.shape
    units = fcw.shape[1]
    base = first // tile
    steps = count // tile
    source = pl.BlockSpec((tile, width), lambda i: (i + base, 0))
    target = pl.BlockSpec((tile, width), lambda i: (i, 0))

    def whole(*shape):
        return pl.BlockSpec(shape, lambda i: (0,) * len(shape))

    return pl.pallas_call(
        feed_kernel,
        grid=(steps,),
        in_specs=[
            pl.BlockSpec(memory_space=pltpu.SMEM),
            source,
            source,
            whole(1, 2 * width + units),
            whole(width, units),
            whole(units, width),
        ]
        + [pl.BlockSpec(memory_space=pl.ANY)] * len(after),
        out_specs=[
            target,
            target,
            whole(units + width, width),
            whole(8, width),
            whole(8, width),
            whole(8, units),
            whole(8, width),
            pl.BlockSpec(memory_space=pltpu.SMEM),
            pl.BlockSpec(memory_space=pl.ANY),
            pl.BlockSpec(memory_space=pl.ANY),
        ],
        out_shape=[
            jax.ShapeDtypeStruct((count, width), BF),
            jax.ShapeDtypeStruct((count, width), BF),
            jax.ShapeDtypeStruct((units + width, width), F32),
            jax.ShapeDtypeStruct((8, width), F32),
            jax.ShapeDtypeStruct((8, width), F32),
            jax.ShapeDtypeStruct((8, units), F32),
            jax.ShapeDtypeStruct((8, width), F32),
            jax.ShapeDtypeStruct((1,), jnp.int32),
            jax.ShapeDtypeStruct((rows, width), BF),
            jax.ShapeDtypeStruct((rows, width), F32),
        ],
        compiler_params=pltpu.CompilerParams(vmem_limit_bytes=VMEM_LIMIT),
        cost_estimate=pl.CostEstimate(flops=1, bytes_accessed=1, transcendentals=0),
        name="feed",
    )(core, tokens, cotangent, vectors, fcw, prw, *after)


def gate_kernel(passed, core, *refs):
    refs[-1][0] = core[0]


def gate(core, ready, passed):
    anywhere = pl.BlockSpec(memory_space=pl.ANY)
    scalar = pl.BlockSpec(memory_space=pltpu.SMEM)
    *handed, stamp = pl.pallas_call(
        functools.partial(gate_kernel, len(passed)),
        in_specs=[scalar] + [anywhere] * (len(passed) + len(ready)),
        out_specs=[anywhere] * len(passed) + [scalar],
        out_shape=[jax.ShapeDtypeStruct(a.shape, a.dtype) for a in passed]
        + [jax.ShapeDtypeStruct((1,), jnp.int32)],
        input_output_aliases={1 + k: k for k in range(len(passed))},
        cost_estimate=pl.CostEstimate(flops=1, bytes_accessed=1, transcendentals=0),
        name="gate",
    )(core, *passed, *ready)
    return handed, stamp[0]


def settle_kernel(core, mine, other, tokens, cotangent, shift, *refs):
    sent, out, grad = refs[-3:]
    total = mine[0].astype(F32) + other[0].astype(F32) + tokens[...].astype(F32) + shift[...]
    out[...] = total.astype(BF)
    sent[0] = total.astype(BF).astype(F32)
    total = mine[1].astype(F32) + other[1].astype(F32) + cotangent[...].astype(F32)
    grad[...] = total
    sent[1] = total


def settle(core, seq, mine, other, tokens, cotangent, shift, outs, after):
    _, half, width = mine.shape
    chunk = half // 2
    stacked = pl.BlockSpec((2, chunk, width), lambda i, core: (0, i, 0))
    rows = pl.BlockSpec((chunk, width), lambda i, core: ((seq * 2 + core[0]) * 2 + i, 0))
    anywhere = pl.BlockSpec(memory_space=pl.ANY)
    return pl.pallas_call(
        settle_kernel,
        grid_spec=pltpu.PrefetchScalarGridSpec(
            num_scalar_prefetch=1,
            grid=(2,),
            in_specs=[stacked, stacked, rows, rows]
            + [pl.BlockSpec((1, width), lambda i, core: (0, 0))]
            + [anywhere] * (2 + len(after)),
            out_specs=[stacked, rows, rows],
        ),
        out_shape=[jax.ShapeDtypeStruct(mine.shape, F32)]
        + [jax.ShapeDtypeStruct(a.shape, a.dtype) for a in outs],
        input_output_aliases={6: 1, 7: 2},
        cost_estimate=pl.CostEstimate(flops=1, bytes_accessed=1, transcendentals=0),
        name="settle",
    )(core, mine, other, tokens, cotangent, shift, *outs, *after)


def place_kernel(core, other, out_before, grad_before, out, grad):
    out[...] = other[0].astype(BF)
    grad[...] = other[1]


def place(core, seq, other, outs):
    _, half, width = other.shape
    chunk = half // 2
    rows = pl.BlockSpec((chunk, width), lambda i, core: ((seq * 2 + 1 - core[0]) * 2 + i, 0))
    return pl.pallas_call(
        place_kernel,
        grid_spec=pltpu.PrefetchScalarGridSpec(
            num_scalar_prefetch=1,
            grid=(2,),
            in_specs=[pl.BlockSpec((2, chunk, width), lambda i, core: (0, i, 0))]
            + [pl.BlockSpec(memory_space=pl.ANY)] * 2,
            out_specs=[rows, rows],
        ),
        out_shape=[jax.ShapeDtypeStruct(a.shape, a.dtype) for a in outs],
        input_output_aliases={2: 0, 3: 1},
        cost_estimate=pl.CostEstimate(flops=1, bytes_accessed=1, transcendentals=0),
        name="place",
    )(core, other, *outs)


def partner(array, lane):
    half = ROT // 2
    width = array.shape[-1]
    return jnp.where(
        lane < half,
        pltpu.roll(array, width - half, 1),
        pltpu.roll(array, half, 1),
    )


def attend_kernel(head, chunk, block, seq, pieces, more, waits, core, *refs):
    tok, cot, ff, e2, gain, shift, wqkv, bqkv, wdense, cosine, sine = refs[:11]
    carried = refs[11 : 11 + 4 * more]
    waits += 4 * more
    tok_hbm, cot_hbm, ff_hbm, e2_hbm = tok, cot, ff, e2
    *refs, tok, cot, ff, e2, sum_s, part_s, in_sem, late_sem, out_sem = refs
    *give, keep, dweights, dgain, dshift, dbqkv, stamp = refs[
        11 + waits : 17 + waits + pieces
    ]
    xhat_s, scale_s, n1_s, q_s, k_s, v_s, dc_s, ctx_s, dm_s, p_s, d_s, dqk_s = refs[17 + waits + pieces :]
    stamp[0] = core[0]
    length, width = tok.shape
    heads = q_s.shape[0]
    first = seq * length

    def fetch(i, k):
        rows = pl.ds(pl.multiple_of(i * chunk, chunk), chunk)
        there = pl.ds(pl.multiple_of(first + i * chunk, chunk), chunk)
        source, target = ((tok_hbm, tok), (cot_hbm, cot))[k]
        return pltpu.make_async_copy(source.at[there, :], target.at[rows, :], in_sem.at[i, k])

    for i in range(length // chunk):
        fetch(i, 0).start()
        fetch(i, 1).start()
    late = [
        pltpu.make_async_copy(ff_hbm.at[pl.ds(first, length), :], ff, late_sem.at[0]),
        pltpu.make_async_copy(e2_hbm.at[pl.ds(first, length), :], e2, late_sem.at[1]),
    ]
    if more:
        late.append(pltpu.make_async_copy(carried[0], sum_s, late_sem.at[2]))
    for copy in late:
        copy.start()

    triple = 3 * head
    half_rows = length // 2
    lane = lax.broadcasted_iota(jnp.int32, (chunk, 2 * head), 1) % head

    def before(i, carry):
        rows = pl.ds(pl.multiple_of(i * chunk, chunk), chunk)
        fetch(i, 0).wait()
        fetch(i, 1).wait()
        xhat, scale = standardise(tok[rows, :].astype(F32))
        xhat_s[rows, :] = xhat
        scale_s[rows, :] = scale
        normed = (xhat * gain[...] + shift[...]).astype(BF)
        n1_s[rows, :] = normed
        cos, sin = cosine[rows, :], sine[rows, :]
        dctx = mm_nt(cot[rows, :], wdense[...]).astype(BF)
        for h in range(heads):
            mixed = mm_nt(normed, wqkv[h * triple : (h + 1) * triple, :]) + bqkv[h : h + 1, :]
            turn = mixed[:, : 2 * head]
            turned = turn * cos + partner(turn, lane) * sin
            q_s[h, rows, :] = (turned[:, :head] * head**-0.5).astype(BF)
            k_s[h, rows, :] = turned[:, head:].astype(BF)
            v_s[h, rows, :] = mixed[:, 2 * head :].astype(BF)
            dc_s[h, rows, :] = dctx[:, h * head : (h + 1) * head]
        return carry

    lax.fori_loop(0, length // chunk, before, 0)

    causal = lax.broadcasted_iota(jnp.int32, (block, block), 1) <= lax.broadcasted_iota(
        jnp.int32, (block, block), 0
    )
    count = length // block

    def one_head(h, carry):
        for i in range(count):
            low, high = i * block, (i + 1) * block
            query = q_s[h, low:high, :]
            dctx = dc_s[h, low:high, :]
            pieces = [(low, high)] if i == 0 else [(0, low), (low, high)]
            scores = []
            for start, stop in pieces:
                part = mm_nt(query, k_s[h, start:stop, :])
                if start == low:
                    part = jnp.where(causal, part, MASKED)
                scores.append(part)
            top = functools.reduce(
                jnp.maximum, [jnp.max(part, axis=-1, keepdims=True) for part in scores]
            )
            scores = [jnp.exp(part - top) for part in scores]
            total = sum(jnp.sum(part, axis=-1, keepdims=True) for part in scores)
            inverse = 1.0 / total
            probs = [part * inverse for part in scores]
            context = 0.0
            for (start, stop), part in zip(pieces, probs):
                rounded = part.astype(BF)
                p_s[low:high, start:stop] = rounded
                context = context + mm(rounded, v_s[h, start:stop, :])
            ctx_s[h, low:high, :] = context.astype(BF)
            inner = jnp.sum(context * dctx.astype(F32), axis=-1, keepdims=True)
            dquery = 0.0
            for (start, stop), part in zip(pieces, probs):
                dprobs = mm_nt(dctx, v_s[h, start:stop, :])
                dscores = (part * (dprobs - inner)).astype(BF)
                d_s[low:high, start:stop] = dscores
                dquery = dquery + mm(dscores, k_s[h, start:stop, :])
            dqk_s[low:high, :head] = dquery * head**-0.5
        for j in range(count):
            low, high = j * block, (j + 1) * block
            dqk_s[low:high, head:] = mm_tn(q_s[h, low:, :], d_s[low:, low:high]).T
            dvalue = mm_tn(dc_s[h, low:, :], p_s[low:, low:high]).T
            dm_s[h, low:high, 2 * head :] = dvalue.astype(BF)
        for j in range(length // chunk):
            low, high = j * chunk, (j + 1) * chunk
            turn = dqk_s[low:high, :]
            back = turn * cosine[low:high, :] - partner(turn, lane) * sine[low:high, :]
            dm_s[h, low:high, : 2 * head] = back.astype(BF)
        return carry

    lax.fori_loop(0, heads, one_head, 0)

    late[0].wait()
    late[1].wait()
    for k, ref in enumerate((dgain, dshift, dbqkv)):
        ref[...] = carried[1 + k][...] if more else jnp.zeros(ref.shape, F32)

    def after(i, carry):
        rows = pl.ds(pl.multiple_of(i * chunk, chunk), chunk)
        context = jnp.concatenate([ctx_s[h, rows, :] for h in range(heads)], axis=-1)
        part = mm(context, wdense[...]) + ff[rows, :].astype(F32)
        dnormed = 0.0
        for h in range(heads):
            dmixed = dm_s[h, rows, :]
            dnormed = dnormed + mm(dmixed, wqkv[h * triple : (h + 1) * triple, :])
            dbqkv[h * 8 : (h + 1) * 8, :] += fold(dmixed.astype(F32))
        xhat, scale = xhat_s[rows, :], scale_s[rows, :]
        dgain[...] += fold(dnormed * xhat)
        dshift[...] += fold(dnormed)
        pulled = dnormed * gain[...] + e2[rows, :].astype(F32)
        mean = jnp.sum(pulled, axis=-1, keepdims=True) * (1.0 / width)
        along = jnp.sum(pulled * xhat, axis=-1, keepdims=True) * (1.0 / width)
        dinput = (scale * (pulled - mean - xhat * along)).astype(BF)
        side = (i * chunk) // half_rows
        there = pl.ds(pl.multiple_of(i * chunk - side * half_rows, chunk), chunk)

        part_s[0, rows, :] = part.astype(BF)
        part_s[1, rows, :] = dinput

        @pl.when(side == core[0])
        def _():
            for k in range(2):
                pltpu.make_async_copy(
                    part_s.at[k, rows, :], keep.at[k, there, :], out_sem.at[i, k]
                ).start()

        size = half_rows * 2 // pieces
        for j in range(pieces // 2):
            within = i * chunk - side * half_rows - j * size

            @pl.when((side != core[0]) & (within >= 0) & (within < size))
            def _():
                spot = pl.ds(pl.multiple_of(within, chunk), chunk)
                for k in range(2):
                    pltpu.make_async_copy(
                        part_s.at[k, rows, :],
                        give[k * (pieces // 2) + j].at[spot, :],
                        out_sem.at[i, k],
                    ).start()

        return carry

    lax.fori_loop(0, length // chunk, after, 0)
    if more:
        late[2].wait()
    for h in range(heads):
        rows = slice(h * triple, (h + 1) * triple)
        part = mm_tn(dm_s[h], n1_s[...])
        dweights[rows, :] = part + sum_s[rows, :] if more else part
        rows = slice(heads * triple + h * head, heads * triple + (h + 1) * head)
        part = mm_tn(ctx_s[h], cot[...])
        dweights[rows, :] = part + sum_s[rows, :] if more else part
    for i in range(length // chunk):
        for k in range(2):
            rows = slice(i * chunk, (i + 1) * chunk)
            pltpu.make_async_copy(
                part_s.at[k, rows, :], keep.at[k, pl.ds(0, chunk), :], out_sem.at[i, k]
            ).wait()


def attend(
    core, tokens, cotangent, ff, e2, gain, shift, wqkv, bqkv, wdense, tables, seq, pieces, carried, after
):
    width = tokens.shape[1]
    heads, triple = bqkv.shape
    head = triple // 3
    chunk, block = 256, 512
    half = LEN // 2

    anywhere = pl.BlockSpec(memory_space=pl.ANY)

    def whole(*shape):
        return pl.BlockSpec(shape, lambda i: (0,) * len(shape))

    sums = [
        whole(4 * heads * head, width),
        whole(8, width),
        whole(8, width),
        whole(8 * heads, triple),
    ]
    return pl.pallas_call(
        functools.partial(attend_kernel, head, chunk, block, seq, pieces, bool(carried), len(after)),
        grid=(1,),
        in_specs=[
            pl.BlockSpec(memory_space=pltpu.SMEM),
            anywhere,
            anywhere,
            anywhere,
            anywhere,
            whole(1, width),
            whole(1, width),
            whole(heads * triple, width),
            whole(heads, triple),
            whole(heads * head, width),
            whole(LEN, 2 * head),
            whole(LEN, 2 * head),
        ]
        + ([anywhere, *sums[1:]] if carried else [])
        + [pl.BlockSpec(memory_space=pl.ANY)] * len(after),
        out_specs=[
            *[anywhere] * pieces,
            anywhere,
            *sums,
            pl.BlockSpec(memory_space=pltpu.SMEM),
        ],
        out_shape=[
            *[jax.ShapeDtypeStruct((2 * half // pieces, width), BF)] * pieces,
            jax.ShapeDtypeStruct((2, half, width), BF),
            jax.ShapeDtypeStruct((4 * heads * head, width), F32),
            jax.ShapeDtypeStruct((8, width), F32),
            jax.ShapeDtypeStruct((8, width), F32),
            jax.ShapeDtypeStruct((8 * heads, triple), F32),
            jax.ShapeDtypeStruct((1,), jnp.int32),
        ],
        scratch_shapes=[
            pltpu.VMEM((LEN, width), F32),
            pltpu.VMEM((LEN, 1), F32),
            pltpu.VMEM((LEN, width), BF),
            pltpu.VMEM((heads, LEN, head), BF),
            pltpu.VMEM((heads, LEN, head), BF),
            pltpu.VMEM((heads, LEN, head), BF),
            pltpu.VMEM((heads, LEN, head), BF),
            pltpu.VMEM((heads, LEN, head), BF),
            pltpu.VMEM((heads, LEN, triple), BF),
            pltpu.VMEM((LEN, LEN), BF),
            pltpu.VMEM((LEN, LEN), BF),
            pltpu.VMEM((LEN, 2 * head), F32),
            *[pltpu.VMEM((LEN, width), BF)] * 4,
            pltpu.VMEM((4 * heads * head, width), F32),
            pltpu.VMEM((2, LEN, width), BF),
            pltpu.SemaphoreType.DMA((LEN // chunk, 2)),
            pltpu.SemaphoreType.DMA((3,)),
            pltpu.SemaphoreType.DMA((LEN // chunk, 2)),
        ],
        compiler_params=pltpu.CompilerParams(vmem_limit_bytes=VMEM_LIMIT),
        cost_estimate=pl.CostEstimate(flops=1, bytes_accessed=1, transcendentals=0),
        name="attend",
    )(core, tokens, cotangent, ff, e2, gain, shift, wqkv, bqkv, wdense, *tables, *carried, *after)


def rotary_tables(head):
    half = ROT // 2
    position = np.arange(LEN, dtype=np.float32)
    inverse = (ROTARY_BASE ** (-(np.arange(half) * 2.0) / ROT)).astype(np.float32)
    angle = (position[:, None] * inverse[None, :]).astype(np.float64)
    cosine = np.ones((LEN, head), np.float32)
    sine = np.zeros((LEN, head), np.float32)
    cosine[:, :half] = cosine[:, half:ROT] = np.cos(angle)
    sine[:, :half] = -np.sin(angle)
    sine[:, half:ROT] = np.sin(angle)
    return np.tile(cosine, (1, 2)), np.tile(sine, (1, 2))


def swap(array, axis, bit):
    size = lax.axis_size(axis)
    return lax.ppermute(array, axis, [(i, i ^ bit) for i in range(size)])


def bits_of(size):
    return [1 << b for b in range(size.bit_length() - 1)]


def span(bits):
    masks = [0]
    for bit in bits:
        masks += [mask | bit for mask in masks]
    return masks


class Sum:
    def __init__(self, array, axis, groups, late):
        self.axis = axis
        self.stages = [(bits, True) for bits in groups]
        self.stages += [(bits, False) for bits in reversed(groups)]
        self.array = array
        self.prepare(late)

    def place(self, bits, late):
        index = lax.axis_index(self.axis) + late
        return sum((((index & bit) != 0).astype(jnp.int32) << k) for k, bit in enumerate(bits))

    def prepare(self, late):
        if not self.stages:
            return
        bits, down = self.stages[0]
        if down:
            size = self.array.shape[0] >> len(bits)
            here = self.place(bits, late)
            self.sent = [
                lax.dynamic_slice_in_dim(self.array, (here ^ k) * size, size, 0).astype(BF)
                for k in range(1, 1 << len(bits))
            ]
        else:
            self.sent = [self.array.astype(BF)]

    def step(self, late):
        bits, down = self.stages.pop(0)
        masks = span(bits)
        here = self.place(bits, late)
        if down:
            size = self.array.shape[0] >> len(bits)
            total = lax.dynamic_slice_in_dim(self.array, here * size, size, 0)
            for mask, sent in zip(masks[1:], self.sent):
                total = total + swap(sent, self.axis, mask).astype(F32)
            self.array = total
        else:
            own = self.sent[0]
            parts = [own] + [swap(own, self.axis, mask) for mask in masks[1:]]
            pieces = []
            for k in range(len(parts)):
                piece = parts[k]
                for other in range(1, len(parts)):
                    piece = jnp.where(here == other, parts[k ^ other], piece)
                pieces.append(piece)
            self.array = jnp.concatenate(pieces, axis=0)
        self.prepare(late)

    def finish(self, late):
        while self.stages:
            self.step(late)
        return self.array.astype(F32)


def sum_doubling(array, axis):
    for bit in bits_of(lax.axis_size(axis)):
        array = array + swap(array, axis, bit)
    return array


def local(
    tokens,
    ln1_gain,
    ln1_bias,
    ln2_gain,
    ln2_bias,
    qkv_weight,
    qkv_bias,
    dense_weight,
    dense_bias,
    fc_weight,
    fc_bias,
    proj_weight,
    proj_bias,
    cotangent,
):
    rows, width = tokens.shape
    heads, triple = qkv_bias.shape
    units = fc_weight.shape[1]
    seqs = rows // LEN
    half = LEN // 2
    core = lax.axis_index("tensor") % 2
    dp_bits = bits_of(lax.axis_size("dp"))
    wqkv = qkv_weight.transpose(1, 2, 0).reshape(heads * triple, width)
    bqkv = qkv_bias.astype(F32)
    tables = rotary_tables(triple // 3)
    row = lambda vector: vector.astype(F32).reshape(1, -1)

    core_ref = core.reshape(1).astype(jnp.int32)

    def attend_rows(s, carried, after):
        *give, keep, a, b, c, d, stamp = attend(
            core_ref,
            tokens,
            cotangent,
            ff,
            e2,
            row(ln1_gain),
            row(ln1_bias),
            wqkv,
            bqkv,
            dense_weight,
            tables,
            s,
            4 if s < seqs - 1 else 2,
            carried,
            after,
        )
        return give, keep, (a, b, c, d), stamp[0]

    def cross(give, keep):
        others = [swap(piece, "tensor", 1) for piece in give]
        n = len(give) // 2
        return jnp.stack(
            [
                            (keep[k].astype(F32) + jnp.concatenate(others[n * k : n * (k + 1)]).astype(F32)).astype(BF)
                for k in range(2)
            ]
        )

    shift = row(dense_bias) + row(proj_bias)

    groups = [(dp_bits[0],), tuple(dp_bits[1:3])] + [(bit,) for bit in dp_bits[3:]]
    ff, e2, dfeed, dgain2, dshift2, dfcb, dbias, stamp, *outs = feed(
        core_ref,
        tokens,
        cotangent,
        row(jnp.concatenate([ln2_gain, ln2_bias, fc_bias])),
        fc_weight,
        proj_weight,
        0,
        rows,
        1024,
    )
    now = stamp[0]
    work = Sum(dfeed, "dp", groups, now - core)
    mine, sent, carried = [], [], ()
    after = tuple(work.sent)

    def settle_rows(s, other, after):
        packet, *into = settle(
            core_ref, s, mine[s], other, tokens, cotangent, shift, outs, after
        )
        return packet, into

    placed = []
    bits = list(dp_bits)
    for s in range(seqs):
        give, keep, carried, now = attend_rows(s, carried, after)
        work.step(now - core)
        ready = list(work.sent)
        if s == seqs - 1:
            packed = Sum(carried[0], "dp", groups, now - core)
            dbqkv = carried[3].reshape(heads, 8, triple).sum(axis=1).reshape(-1)
            vectors = [carried[1].sum(0), carried[2].sum(0), dgain2.sum(0), dshift2.sum(0)]
            vectors += [dfcb.sum(0), dbias.sum(0), dbqkv]
            sizes = [vector.shape[0] for vector in vectors]
            lanes = 1024
            flat = jnp.concatenate(vectors + [jnp.zeros((-sum(sizes) % lanes,), F32)])
            flat = flat.reshape(-1, lanes)
            placed = [swap(packet, "tensor", 1) for packet in sent]
            ready += [*packed.sent, *placed]
        give, _ = gate(core_ref, ready, give)
        if s >= 1:
            other = swap(mine[s - 1], "tensor", 2)
            (keep,), now = gate(core_ref, [other], [keep])
        mine.append(cross(give, keep))
        after = (mine[s], *work.sent)
        if s == seqs - 1:
            _, stamp = gate(core_ref, [mine[s]], [])
            packed.step(stamp - core)
            after += tuple(packed.sent)
        if s >= 1:
            packet, outs = settle_rows(s - 1, other, after)
            sent.append(packet)
            after += (packet,)

    handed, stamp = gate(core_ref, packed.sent, [*work.sent, flat])
    *work.sent, flat = handed
    for s, packet in enumerate(placed):
        outs = place(core_ref, s, packet, outs)
    if packed.stages:
        packed.step(stamp - core)
    if packed.stages:
        packed.step(stamp - core)
    other = swap(mine[-1], "tensor", 2)
    _, stamp = gate(core_ref, [other], [])
    both = work.finish(stamp - core)
    dproj, dfc = both[:units], both[units:]
    packet, outs = settle_rows(seqs - 1, other, (*packed.sent, dproj, dfc))
    (flat, *last), stamp = gate(core_ref, [packet], [flat, *sent[len(placed) :]])
    for bit in bits[1:]:
        flat = flat + swap(flat, "dp", bit)
    for s, each in enumerate(last):
        outs = place(core_ref, len(placed) + s, swap(each, "tensor", 1), outs)
    (flat,), _ = gate(core_ref, outs, [flat])
    last = [packet]
    norms = flat.reshape(-1)[: 4 * width].reshape(4, width)
    norms = norms + swap(norms, "tensor", 1)
    norms = norms + swap(norms, "tensor", 2)
    norms = norms + swap(norms, "dp", bits[0])
    flat = flat + swap(flat, "dp", bits[0])
    for s, each in enumerate(last):
        outs = place(core_ref, seqs - 1, swap(each, "tensor", 1), outs)
    block_out, input_grad = outs
    packed = packed.finish(stamp - core)
    flat = flat.reshape(-1)
    dqkv = packed[: heads * triple].reshape(heads, triple, width).transpose(2, 0, 1)
    ddense = packed[heads * triple :]

    offsets = np.cumsum([0] + sizes)
    dfcb, dbias, dbqkv = [flat[offsets[i] : offsets[i + 1]] for i in (4, 5, 6)]
    return (
        block_out,
        input_grad,
        norms[0],
        norms[1],
        norms[2],
        norms[3],
        dqkv,
        dbqkv.reshape(heads, triple),
        ddense,
        dbias,
        dfc,
        dfcb,
        dproj,
        dbias,
    )


def solution(mesh):
    in_specs = (
        P("dp", None),
        P(),
        P(),
        P(),
        P(),
        P(None, "tensor", None),
        P("tensor", None),
        P("tensor", None),
        P(),
        P(None, "tensor"),
        P("tensor"),
        P("tensor", None),
        P(),
        P("dp", None),
    )
    out_specs = (
        P("dp", None),
        P("dp", None),
        P(),
        P(),
        P(),
        P(),
        P(None, "tensor", None),
        P("tensor", None),
        P("tensor", None),
        P(),
        P(None, "tensor"),
        P("tensor"),
        P("tensor", None),
        P(),
    )
    return jax.shard_map(local, mesh=mesh, in_specs=in_specs, out_specs=out_specs, check_vma=False)
```

```python
import functools

import jax
import jax.numpy as jnp
import numpy as np
from jax import lax
from jax.experimental import pallas as pl
from jax.experimental.pallas import tpu as pltpu
from jax.sharding import PartitionSpec as P

ROT = 16
LEN = 1024
EPSILON = 1e-05
ROTARY_BASE = 10000.0
MASKED = -1e30
VMEM_LIMIT = 56 * 1024 * 1024
BF = jnp.bfloat16
F32 = jnp.float32


def mm(a, b):
    return lax.dot_general(a, b, (((1,), (0,)), ((), ())), preferred_element_type=F32)


def mm_nt(a, b):
    return lax.dot_general(a, b, (((1,), (1,)), ((), ())), preferred_element_type=F32)


def mm_tn(a, b):
    return lax.dot_general(a, b, (((0,), (0,)), ((), ())), preferred_element_type=F32)


def fold(array):
    rows, width = array.shape
    return jnp.sum(array.reshape(rows // 8, 8, width), axis=0)


def standardise(rows):
    width = rows.shape[-1]
    centred = rows - jnp.sum(rows, axis=-1, keepdims=True) * (1.0 / width)
    spread = jnp.sum(centred * centred, axis=-1, keepdims=True) * (1.0 / width)
    scale = lax.rsqrt(spread + EPSILON)
    return centred * scale, scale


def gelu_parts(value):
    phi = 0.5 + 0.5 * lax.erf(value * 0.7071067811865476)
    bell = jnp.exp(value * value * -0.5)
    return value * phi, phi + value * bell * 0.3989422804014327


def feed_kernel(core, tok, cot, vectors, fcw, prw, *rest):
    ff, e2, dweights, dgain, dshift, dfcb, dbias, stamp, _, _ = rest[-10:]
    width, units = fcw.shape
    gain, shift = vectors[:, :width], vectors[:, width : 2 * width]
    step = pl.program_id(0)
    stamp[0] = core[0]
    xhat, _ = standardise(tok[...].astype(F32))
    normed = (xhat * gain + shift).astype(BF)
    hidden = mm(normed, fcw[...]) + vectors[:, 2 * width :]
    act, slope = gelu_parts(hidden)
    act = act.astype(BF)
    upstream = cot[...]
    ff[...] = mm(act, prw[...]).astype(BF)
    dhidden = (mm_nt(upstream, prw[...]) * slope).astype(BF)
    dnormed = mm_nt(dhidden, fcw[...])
    e2[...] = (dnormed * gain).astype(BF)

    @pl.when(step == 0)
    def _():
        for ref in (dweights, dgain, dshift, dfcb, dbias):
            ref[...] = jnp.zeros(ref.shape, F32)

    dweights[:units, :] += mm_tn(act, upstream)
    dweights[units:, :] += mm_tn(normed, dhidden)
    dgain[...] += fold(dnormed * xhat)
    dshift[...] += fold(dnormed)
    dfcb[...] += fold(dhidden.astype(F32))
    dbias[...] += fold(upstream.astype(F32))


def feed(core, tokens, cotangent, vectors, fcw, prw, first, count, tile, after=()):
    rows, width = tokens.shape
    units = fcw.shape[1]
    base = first // tile
    steps = count // tile
    source = pl.BlockSpec((tile, width), lambda i: (i + base, 0))
    target = pl.BlockSpec((tile, width), lambda i: (i, 0))

    def whole(*shape):
        return pl.BlockSpec(shape, lambda i: (0,) * len(shape))

    return pl.pallas_call(
        feed_kernel,
        grid=(steps,),
        in_specs=[
            pl.BlockSpec(memory_space=pltpu.SMEM),
            source,
            source,
            whole(1, 2 * width + units),
            whole(width, units),
            whole(units, width),
        ]
        + [pl.BlockSpec(memory_space=pl.ANY)] * len(after),
        out_specs=[
            target,
            target,
            whole(units + width, width),
            whole(8, width),
            whole(8, width),
            whole(8, units),
            whole(8, width),
            pl.BlockSpec(memory_space=pltpu.SMEM),
            pl.BlockSpec(memory_space=pl.ANY),
            pl.BlockSpec(memory_space=pl.ANY),
        ],
        out_shape=[
            jax.ShapeDtypeStruct((count, width), BF),
            jax.ShapeDtypeStruct((count, width), BF),
            jax.ShapeDtypeStruct((units + width, width), F32),
            jax.ShapeDtypeStruct((8, width), F32),
            jax.ShapeDtypeStruct((8, width), F32),
            jax.ShapeDtypeStruct((8, units), F32),
            jax.ShapeDtypeStruct((8, width), F32),
            jax.ShapeDtypeStruct((1,), jnp.int32),
            jax.ShapeDtypeStruct((rows, width), BF),
            jax.ShapeDtypeStruct((rows, width), F32),
        ],
        compiler_params=pltpu.CompilerParams(vmem_limit_bytes=VMEM_LIMIT),
        cost_estimate=pl.CostEstimate(flops=1, bytes_accessed=1, transcendentals=0),
        name="feed",
    )(core, tokens, cotangent, vectors, fcw, prw, *after)


def gate_kernel(passed, core, *refs):
    refs[-1][0] = core[0]


def gate(core, ready, passed):
    anywhere = pl.BlockSpec(memory_space=pl.ANY)
    scalar = pl.BlockSpec(memory_space=pltpu.SMEM)
    *handed, stamp = pl.pallas_call(
        functools.partial(gate_kernel, len(passed)),
        in_specs=[scalar] + [anywhere] * (len(passed) + len(ready)),
        out_specs=[anywhere] * len(passed) + [scalar],
        out_shape=[jax.ShapeDtypeStruct(a.shape, a.dtype) for a in passed]
        + [jax.ShapeDtypeStruct((1,), jnp.int32)],
        input_output_aliases={1 + k: k for k in range(len(passed))},
        cost_estimate=pl.CostEstimate(flops=1, bytes_accessed=1, transcendentals=0),
        name="gate",
    )(core, *passed, *ready)
    return handed, stamp[0]


def settle_kernel(core, mine, other, tokens, cotangent, shift, *refs):
    sent, out, grad = refs[-3:]
    total = mine[0].astype(F32) + other[0].astype(F32) + tokens[...].astype(F32) + shift[...]
    out[...] = total.astype(BF)
    sent[0] = total.astype(BF).astype(F32)
    total = mine[1].astype(F32) + other[1].astype(F32) + cotangent[...].astype(F32)
    grad[...] = total
    sent[1] = total


def settle(core, seq, mine, other, tokens, cotangent, shift, outs, after):
    _, half, width = mine.shape
    chunk = half // 2
    stacked = pl.BlockSpec((2, chunk, width), lambda i, core: (0, i, 0))
    rows = pl.BlockSpec((chunk, width), lambda i, core: ((seq * 2 + core[0]) * 2 + i, 0))
    anywhere = pl.BlockSpec(memory_space=pl.ANY)
    return pl.pallas_call(
        settle_kernel,
        grid_spec=pltpu.PrefetchScalarGridSpec(
            num_scalar_prefetch=1,
            grid=(2,),
            in_specs=[stacked, stacked, rows, rows]
            + [pl.BlockSpec((1, width), lambda i, core: (0, 0))]
            + [anywhere] * (2 + len(after)),
            out_specs=[stacked, rows, rows],
        ),
        out_shape=[jax.ShapeDtypeStruct(mine.shape, F32)]
        + [jax.ShapeDtypeStruct(a.shape, a.dtype) for a in outs],
        input_output_aliases={6: 1, 7: 2},
        cost_estimate=pl.CostEstimate(flops=1, bytes_accessed=1, transcendentals=0),
        name="settle",
    )(core, mine, other, tokens, cotangent, shift, *outs, *after)


def place_kernel(core, other, out_before, grad_before, out, grad):
    out[...] = other[0].astype(BF)
    grad[...] = other[1]


def place(core, seq, other, outs):
    _, half, width = other.shape
    chunk = half // 2
    rows = pl.BlockSpec((chunk, width), lambda i, core: ((seq * 2 + 1 - core[0]) * 2 + i, 0))
    return pl.pallas_call(
        place_kernel,
        grid_spec=pltpu.PrefetchScalarGridSpec(
            num_scalar_prefetch=1,
            grid=(2,),
            in_specs=[pl.BlockSpec((2, chunk, width), lambda i, core: (0, i, 0))]
            + [pl.BlockSpec(memory_space=pl.ANY)] * 2,
            out_specs=[rows, rows],
        ),
        out_shape=[jax.ShapeDtypeStruct(a.shape, a.dtype) for a in outs],
        input_output_aliases={2: 0, 3: 1},
        cost_estimate=pl.CostEstimate(flops=1, bytes_accessed=1, transcendentals=0),
        name="place",
    )(core, other, *outs)


def partner(array, lane):
    half = ROT // 2
    width = array.shape[-1]
    return jnp.where(
        lane < half,
        pltpu.roll(array, width - half, 1),
        pltpu.roll(array, half, 1),
    )


def attend_kernel(head, chunk, block, seq, pieces, more, waits, core, *refs):
    tok, cot, ff, e2, gain, shift, wqkv, bqkv, wdense, cosine, sine = refs[:11]
    carried = refs[11 : 11 + 4 * more]
    waits += 4 * more
    tok_hbm, cot_hbm, ff_hbm, e2_hbm = tok, cot, ff, e2
    *refs, tok, cot, ff, e2, sum_s, part_s, in_sem, late_sem, out_sem = refs
    *give, keep, dweights, dgain, dshift, dbqkv, stamp = refs[
        11 + waits : 17 + waits + pieces
    ]
    xhat_s, scale_s, n1_s, q_s, k_s, v_s, dc_s, ctx_s, dm_s, p_s, d_s, dqk_s = refs[17 + waits + pieces :]
    stamp[0] = core[0]
    length, width = tok.shape
    heads = q_s.shape[0]
    first = seq * length

    def fetch(i, k):
        rows = pl.ds(pl.multiple_of(i * chunk, chunk), chunk)
        there = pl.ds(pl.multiple_of(first + i * chunk, chunk), chunk)
        source, target = ((tok_hbm, tok), (cot_hbm, cot))[k]
        return pltpu.make_async_copy(source.at[there, :], target.at[rows, :], in_sem.at[i, k])

    for i in range(length // chunk):
        fetch(i, 0).start()
        fetch(i, 1).start()
    late = [
        pltpu.make_async_copy(ff_hbm.at[pl.ds(first, length), :], ff, late_sem.at[0]),
        pltpu.make_async_copy(e2_hbm.at[pl.ds(first, length), :], e2, late_sem.at[1]),
    ]
    if more:
        late.append(pltpu.make_async_copy(carried[0], sum_s, late_sem.at[2]))
    for copy in late:
        copy.start()

    triple = 3 * head
    half_rows = length // 2
    lane = lax.broadcasted_iota(jnp.int32, (chunk, 2 * head), 1) % head

    def before(i, carry):
        rows = pl.ds(pl.multiple_of(i * chunk, chunk), chunk)
        fetch(i, 0).wait()
        fetch(i, 1).wait()
        xhat, scale = standardise(tok[rows, :].astype(F32))
        xhat_s[rows, :] = xhat
        scale_s[rows, :] = scale
        normed = (xhat * gain[...] + shift[...]).astype(BF)
        n1_s[rows, :] = normed
        cos, sin = cosine[rows, :], sine[rows, :]
        dctx = mm_nt(cot[rows, :], wdense[...]).astype(BF)
        for h in range(heads):
            mixed = mm_nt(normed, wqkv[h * triple : (h + 1) * triple, :]) + bqkv[h : h + 1, :]
            turn = mixed[:, : 2 * head]
            turned = turn * cos + partner(turn, lane) * sin
            q_s[h, rows, :] = (turned[:, :head] * head**-0.5).astype(BF)
            k_s[h, rows, :] = turned[:, head:].astype(BF)
            v_s[h, rows, :] = mixed[:, 2 * head :].astype(BF)
            dc_s[h, rows, :] = dctx[:, h * head : (h + 1) * head]
        return carry

    lax.fori_loop(0, length // chunk, before, 0)

    causal = lax.broadcasted_iota(jnp.int32, (block, block), 1) <= lax.broadcasted_iota(
        jnp.int32, (block, block), 0
    )
    count = length // block

    def one_head(h, carry):
        for i in range(count):
            low, high = i * block, (i + 1) * block
            query = q_s[h, low:high, :]
            dctx = dc_s[h, low:high, :]
            pieces = [(low, high)] if i == 0 else [(0, low), (low, high)]
            scores = []
            for start, stop in pieces:
                part = mm_nt(query, k_s[h, start:stop, :])
                if start == low:
                    part = jnp.where(causal, part, MASKED)
                scores.append(part)
            top = functools.reduce(
                jnp.maximum, [jnp.max(part, axis=-1, keepdims=True) for part in scores]
            )
            scores = [jnp.exp(part - top) for part in scores]
            total = sum(jnp.sum(part, axis=-1, keepdims=True) for part in scores)
            inverse = 1.0 / total
            probs = [part * inverse for part in scores]
            context = 0.0
            for (start, stop), part in zip(pieces, probs):
                rounded = part.astype(BF)
                p_s[low:high, start:stop] = rounded
                context = context + mm(rounded, v_s[h, start:stop, :])
            ctx_s[h, low:high, :] = context.astype(BF)
            inner = jnp.sum(context * dctx.astype(F32), axis=-1, keepdims=True)
            dquery = 0.0
            for (start, stop), part in zip(pieces, probs):
                dprobs = mm_nt(dctx, v_s[h, start:stop, :])
                dscores = (part * (dprobs - inner)).astype(BF)
                d_s[low:high, start:stop] = dscores
                dquery = dquery + mm(dscores, k_s[h, start:stop, :])
            dqk_s[low:high, :head] = dquery * head**-0.5
        for j in range(count):
            low, high = j * block, (j + 1) * block
            dqk_s[low:high, head:] = mm_tn(q_s[h, low:, :], d_s[low:, low:high]).T
            dvalue = mm_tn(dc_s[h, low:, :], p_s[low:, low:high]).T
            dm_s[h, low:high, 2 * head :] = dvalue.astype(BF)
        for j in range(length // chunk):
            low, high = j * chunk, (j + 1) * chunk
            turn = dqk_s[low:high, :]
            back = turn * cosine[low:high, :] - partner(turn, lane) * sine[low:high, :]
            dm_s[h, low:high, : 2 * head] = back.astype(BF)
        return carry

    for h in range(heads):
        one_head(h, 0)

    late[0].wait()
    late[1].wait()
    for k, ref in enumerate((dgain, dshift, dbqkv)):
        ref[...] = carried[1 + k][...] if more else jnp.zeros(ref.shape, F32)

    def after(i, carry):
        rows = pl.ds(pl.multiple_of(i * chunk, chunk), chunk)
        context = jnp.concatenate([ctx_s[h, rows, :] for h in range(heads)], axis=-1)
        part = mm(context, wdense[...]) + ff[rows, :].astype(F32)
        dnormed = 0.0
        for h in range(heads):
            dmixed = dm_s[h, rows, :]
            dnormed = dnormed + mm(dmixed, wqkv[h * triple : (h + 1) * triple, :])
            dbqkv[h * 8 : (h + 1) * 8, :] += fold(dmixed.astype(F32))
        xhat, scale = xhat_s[rows, :], scale_s[rows, :]
        dgain[...] += fold(dnormed * xhat)
        dshift[...] += fold(dnormed)
        pulled = dnormed * gain[...] + e2[rows, :].astype(F32)
        mean = jnp.sum(pulled, axis=-1, keepdims=True) * (1.0 / width)
        along = jnp.sum(pulled * xhat, axis=-1, keepdims=True) * (1.0 / width)
        dinput = (scale * (pulled - mean - xhat * along)).astype(BF)
        side = (i * chunk) // half_rows
        there = pl.ds(pl.multiple_of(i * chunk - side * half_rows, chunk), chunk)

        part_s[0, rows, :] = part.astype(BF)
        part_s[1, rows, :] = dinput

        @pl.when(side == core[0])
        def _():
            for k in range(2):
                pltpu.make_async_copy(
                    part_s.at[k, rows, :], keep.at[k, there, :], out_sem.at[i, k]
                ).start()

        size = half_rows * 2 // pieces
        for j in range(pieces // 2):
            within = i * chunk - side * half_rows - j * size

            @pl.when((side != core[0]) & (within >= 0) & (within < size))
            def _():
                spot = pl.ds(pl.multiple_of(within, chunk), chunk)
                for k in range(2):
                    pltpu.make_async_copy(
                        part_s.at[k, rows, :],
                        give[k * (pieces // 2) + j].at[spot, :],
                        out_sem.at[i, k],
                    ).start()

        return carry

    lax.fori_loop(0, length // chunk, after, 0)
    if more:
        late[2].wait()
    for h in range(heads):
        rows = slice(h * triple, (h + 1) * triple)
        part = mm_tn(dm_s[h], n1_s[...])
        dweights[rows, :] = part + sum_s[rows, :] if more else part
        rows = slice(heads * triple + h * head, heads * triple + (h + 1) * head)
        part = mm_tn(ctx_s[h], cot[...])
        dweights[rows, :] = part + sum_s[rows, :] if more else part
    for i in range(length // chunk):
        for k in range(2):
            rows = slice(i * chunk, (i + 1) * chunk)
            pltpu.make_async_copy(
                part_s.at[k, rows, :], keep.at[k, pl.ds(0, chunk), :], out_sem.at[i, k]
            ).wait()


def attend(
    core, tokens, cotangent, ff, e2, gain, shift, wqkv, bqkv, wdense, tables, seq, pieces, carried, after
):
    width = tokens.shape[1]
    heads, triple = bqkv.shape
    head = triple // 3
    chunk, block = 256, 512
    half = LEN // 2

    anywhere = pl.BlockSpec(memory_space=pl.ANY)

    def whole(*shape):
        return pl.BlockSpec(shape, lambda i: (0,) * len(shape))

    sums = [
        whole(4 * heads * head, width),
        whole(8, width),
        whole(8, width),
        whole(8 * heads, triple),
    ]
    return pl.pallas_call(
        functools.partial(attend_kernel, head, chunk, block, seq, pieces, bool(carried), len(after)),
        grid=(1,),
        in_specs=[
            pl.BlockSpec(memory_space=pltpu.SMEM),
            anywhere,
            anywhere,
            anywhere,
            anywhere,
            whole(1, width),
            whole(1, width),
            whole(heads * triple, width),
            whole(heads, triple),
            whole(heads * head, width),
            whole(LEN, 2 * head),
            whole(LEN, 2 * head),
        ]
        + ([anywhere, *sums[1:]] if carried else [])
        + [pl.BlockSpec(memory_space=pl.ANY)] * len(after),
        out_specs=[
            *[anywhere] * pieces,
            anywhere,
            *sums,
            pl.BlockSpec(memory_space=pltpu.SMEM),
        ],
        out_shape=[
            *[jax.ShapeDtypeStruct((2 * half // pieces, width), BF)] * pieces,
            jax.ShapeDtypeStruct((2, half, width), BF),
            jax.ShapeDtypeStruct((4 * heads * head, width), F32),
            jax.ShapeDtypeStruct((8, width), F32),
            jax.ShapeDtypeStruct((8, width), F32),
            jax.ShapeDtypeStruct((8 * heads, triple), F32),
            jax.ShapeDtypeStruct((1,), jnp.int32),
        ],
        scratch_shapes=[
            pltpu.VMEM((LEN, width), F32),
            pltpu.VMEM((LEN, 1), F32),
            pltpu.VMEM((LEN, width), BF),
            pltpu.VMEM((heads, LEN, head), BF),
            pltpu.VMEM((heads, LEN, head), BF),
            pltpu.VMEM((heads, LEN, head), BF),
            pltpu.VMEM((heads, LEN, head), BF),
            pltpu.VMEM((heads, LEN, head), BF),
            pltpu.VMEM((heads, LEN, triple), BF),
            pltpu.VMEM((LEN, LEN), BF),
            pltpu.VMEM((LEN, LEN), BF),
            pltpu.VMEM((LEN, 2 * head), F32),
            *[pltpu.VMEM((LEN, width), BF)] * 4,
            pltpu.VMEM((4 * heads * head, width), F32),
            pltpu.VMEM((2, LEN, width), BF),
            pltpu.SemaphoreType.DMA((LEN // chunk, 2)),
            pltpu.SemaphoreType.DMA((3,)),
            pltpu.SemaphoreType.DMA((LEN // chunk, 2)),
        ],
        compiler_params=pltpu.CompilerParams(vmem_limit_bytes=VMEM_LIMIT),
        cost_estimate=pl.CostEstimate(flops=1, bytes_accessed=1, transcendentals=0),
        name="attend",
    )(core, tokens, cotangent, ff, e2, gain, shift, wqkv, bqkv, wdense, *tables, *carried, *after)


def rotary_tables(head):
    half = ROT // 2
    position = np.arange(LEN, dtype=np.float32)
    inverse = (ROTARY_BASE ** (-(np.arange(half) * 2.0) / ROT)).astype(np.float32)
    angle = (position[:, None] * inverse[None, :]).astype(np.float64)
    cosine = np.ones((LEN, head), np.float32)
    sine = np.zeros((LEN, head), np.float32)
    cosine[:, :half] = cosine[:, half:ROT] = np.cos(angle)
    sine[:, :half] = -np.sin(angle)
    sine[:, half:ROT] = np.sin(angle)
    return np.tile(cosine, (1, 2)), np.tile(sine, (1, 2))


def swap(array, axis, bit):
    size = lax.axis_size(axis)
    return lax.ppermute(array, axis, [(i, i ^ bit) for i in range(size)])


def bits_of(size):
    return [1 << b for b in range(size.bit_length() - 1)]


def span(bits):
    masks = [0]
    for bit in bits:
        masks += [mask | bit for mask in masks]
    return masks


class Sum:
    def __init__(self, array, axis, groups, late):
        self.axis = axis
        self.stages = [(bits, True) for bits in groups]
        self.stages += [(bits, False) for bits in reversed(groups)]
        self.array = array
        self.received = []
        self.prepare(late)

    def place(self, bits, late):
        index = lax.axis_index(self.axis) + late
        return sum((((index & bit) != 0).astype(jnp.int32) << k) for k, bit in enumerate(bits))

    def prepare(self, late):
        if not self.stages:
            return
        bits, down = self.stages[0]
        if down:
            size = self.array.shape[0] >> len(bits)
            here = self.place(bits, late)
            self.sent = [
                lax.dynamic_slice_in_dim(self.array, (here ^ k) * size, size, 0).astype(BF)
                for k in range(1, 1 << len(bits))
            ]
        else:
            self.sent = [self.array.astype(BF)]

    def receive(self):
        bits, down = self.stages[0]
        masks = span(bits)[1:]
        sent = self.sent if down else self.sent * len(masks)
        self.received = [swap(part, self.axis, mask) for part, mask in zip(sent, masks)]
        return self.received

    def step(self, late):
        if not self.received:
            self.receive()
        bits, down = self.stages.pop(0)
        received, self.received = self.received, []
        here = self.place(bits, late)
        if down:
            size = self.array.shape[0] >> len(bits)
            total = lax.dynamic_slice_in_dim(self.array, here * size, size, 0)
            for part in received:
                total = total + part.astype(F32)
            self.array = total
        else:
            own = self.sent[0]
            parts = [own] + received
            pieces = []
            for k in range(len(parts)):
                piece = parts[k]
                for other in range(1, len(parts)):
                    piece = jnp.where(here == other, parts[k ^ other], piece)
                pieces.append(piece)
            self.array = jnp.concatenate(pieces, axis=0)
        self.prepare(late)

    def finish(self, late):
        while self.stages:
            self.step(late)
        return self.array.astype(F32)


def sum_doubling(array, axis):
    for bit in bits_of(lax.axis_size(axis)):
        array = array + swap(array, axis, bit)
    return array


def local(
    tokens,
    ln1_gain,
    ln1_bias,
    ln2_gain,
    ln2_bias,
    qkv_weight,
    qkv_bias,
    dense_weight,
    dense_bias,
    fc_weight,
    fc_bias,
    proj_weight,
    proj_bias,
    cotangent,
):
    rows, width = tokens.shape
    heads, triple = qkv_bias.shape
    units = fc_weight.shape[1]
    seqs = rows // LEN
    half = LEN // 2
    core = lax.axis_index("tensor") % 2
    dp_bits = bits_of(lax.axis_size("dp"))
    wqkv = qkv_weight.transpose(1, 2, 0).reshape(heads * triple, width)
    bqkv = qkv_bias.astype(F32)
    tables = rotary_tables(triple // 3)
    row = lambda vector: vector.astype(F32).reshape(1, -1)

    core_ref = core.reshape(1).astype(jnp.int32)

    def attend_rows(s, carried, after):
        *give, keep, a, b, c, d, stamp = attend(
            core_ref,
            tokens,
            cotangent,
            ff,
            e2,
            row(ln1_gain),
            row(ln1_bias),
            wqkv,
            bqkv,
            dense_weight,
            tables,
            s,
            4 if s < seqs - 1 else 2,
            carried,
            after,
        )
        return give, keep, (a, b, c, d), stamp[0]

    def cross(give, keep):
        others = [swap(piece, "tensor", 1) for piece in give]
        n = len(give) // 2
        return jnp.stack(
            [
                (keep[k].astype(F32) + jnp.concatenate(others[n * k : n * (k + 1)]).astype(F32)).astype(BF)
                for k in range(2)
            ]
        )

    shift = row(dense_bias) + row(proj_bias)

    groups = [(dp_bits[0],), tuple(dp_bits[1:3])] + [(bit,) for bit in dp_bits[3:]]
    ff, e2, dfeed, dgain2, dshift2, dfcb, dbias, stamp, *outs = feed(
        core_ref,
        tokens,
        cotangent,
        row(jnp.concatenate([ln2_gain, ln2_bias, fc_bias])),
        fc_weight,
        proj_weight,
        0,
        rows,
        1024,
    )
    now = stamp[0]
    work = Sum(dfeed, "dp", groups, now - core)
    mine, sent, carried = [], [], ()
    after = tuple(work.sent)

    def settle_rows(s, other, after):
        packet, *into = settle(
            core_ref, s, mine[s], other, tokens, cotangent, shift, outs, after
        )
        return packet, into

    pending = []
    bits = list(dp_bits)
    for s in range(seqs):
        give, keep, carried, now = attend_rows(s, carried, after)
        if s < seqs - 1:
            work.step(now - core)
            ready = list(work.sent)
        else:
            ready = list(work.receive())
            packed = Sum(carried[0], "dp", groups, now - core)
            dbqkv = carried[3].reshape(heads, 8, triple).sum(axis=1).reshape(-1)
            vectors = [carried[1].sum(0), carried[2].sum(0), dgain2.sum(0), dshift2.sum(0)]
            vectors += [dfcb.sum(0), dbias.sum(0), dbqkv]
            sizes = [vector.shape[0] for vector in vectors]
            lanes = 1024
            flat = jnp.concatenate(vectors + [jnp.zeros((-sum(sizes) % lanes,), F32)])
            flat = flat.reshape(-1, lanes)
            ready += packed.sent
        give, _ = gate(core_ref, ready, give)
        if s >= 1:
            other = swap(mine[s - 1], "tensor", 2)
            (keep,), now = gate(core_ref, [other], [keep])
        mine.append(cross(give, keep))
        if s == seqs - 1:
            _, stamp = gate(core_ref, [mine[s]], [])
            packed.step(stamp - core)
            work.step(stamp - core)
        after = (mine[s], *work.sent)
        if s >= 1:
            pending.append(other)

    handed, stamp = gate(core_ref, packed.sent, [*work.sent, flat])
    *work.sent, flat = handed
    for s, other in enumerate(pending):
        packet, outs = settle_rows(s, other, tuple(packed.sent))
        sent.append(packet)
    _, stamp = gate(core_ref, [sent[-1]] if sent else [], [])
    if packed.stages:
        packed.step(stamp - core)
    if packed.stages:
        packed.step(stamp - core)
    other = swap(mine[-1], "tensor", 2)
    _, stamp = gate(core_ref, [other], [])
    both = work.finish(stamp - core)
    dproj, dfc = both[:units], both[units:]
    packet, outs = settle_rows(seqs - 1, other, (*packed.sent, dproj, dfc))
    (flat, *last), stamp = gate(core_ref, [packet], [flat, *sent])
    packets = [swap(each, "tensor", 1) for each in last]

    def beside(array, axis, bit):
        nonlocal outs
        other = swap(array, axis, bit)
        if packets:
            outs = place(core_ref, seqs - 1 - len(packets), packets.pop(0), outs)
            (other,), _ = gate(core_ref, outs, [other])
        return array + other

    flat = flat + swap(flat, "dp", bits[1]) if bits[1:] else flat
    for bit in bits[2:]:
        flat = beside(flat, "dp", bit)
    last = [packet]
    norms = flat.reshape(-1)[: 4 * width].reshape(4, width)
    norms = beside(norms, "tensor", 1)
    norms = beside(norms, "tensor", 2)
    while packets:
        outs = place(core_ref, seqs - 1 - len(packets), packets.pop(0), outs)
    (norms, flat), stamp = gate(core_ref, outs, [norms, flat])
    norms = norms + swap(norms, "dp", bits[0])
    flat = flat + swap(flat, "dp", bits[0])
    for s, each in enumerate(last):
        outs = place(core_ref, seqs - 1, swap(each, "tensor", 1), outs)
    block_out, input_grad = outs
    packed = packed.finish(stamp - core)
    flat = flat.reshape(-1)
    dqkv = packed[: heads * triple].reshape(heads, triple, width).transpose(2, 0, 1)
    ddense = packed[heads * triple :]

    offsets = np.cumsum([0] + sizes)
    dfcb, dbias, dbqkv = [flat[offsets[i] : offsets[i + 1]] for i in (4, 5, 6)]
    return (
        block_out,
        input_grad,
        norms[0],
        norms[1],
        norms[2],
        norms[3],
        dqkv,
        dbqkv.reshape(heads, triple),
        ddense,
        dbias,
        dfc,
        dfcb,
        dproj,
        dbias,
    )


def solution(mesh):
    in_specs = (
        P("dp", None),
        P(),
        P(),
        P(),
        P(),
        P(None, "tensor", None),
        P("tensor", None),
        P("tensor", None),
        P(),
        P(None, "tensor"),
        P("tensor"),
        P("tensor", None),
        P(),
        P("dp", None),
    )
    out_specs = (
        P("dp", None),
        P("dp", None),
        P(),
        P(),
        P(),
        P(),
        P(None, "tensor", None),
        P("tensor", None),
        P("tensor", None),
        P(),
        P(None, "tensor"),
        P("tensor"),
        P("tensor", None),
        P(),
    )
    return jax.shard_map(local, mesh=mesh, in_specs=in_specs, out_specs=out_specs, check_vma=False)
```

```python
import functools

import jax
import jax.numpy as jnp
import numpy as np
from jax import lax
from jax.experimental import pallas as pl
from jax.experimental.pallas import tpu as pltpu
from jax.sharding import PartitionSpec as P

ROT = 16
LEN = 1024
EPSILON = 1e-05
ROTARY_BASE = 10000.0
MASKED = -1e30
VMEM_LIMIT = 56 * 1024 * 1024
BF = jnp.bfloat16
F32 = jnp.float32


def mm(a, b):
    return lax.dot_general(a, b, (((1,), (0,)), ((), ())), preferred_element_type=F32)


def mm_nt(a, b):
    return lax.dot_general(a, b, (((1,), (1,)), ((), ())), preferred_element_type=F32)


def mm_tn(a, b):
    return lax.dot_general(a, b, (((0,), (0,)), ((), ())), preferred_element_type=F32)


def fold(array):
    rows, width = array.shape
    return jnp.sum(array.reshape(rows // 8, 8, width), axis=0)


def standardise(rows):
    width = rows.shape[-1]
    centred = rows - jnp.sum(rows, axis=-1, keepdims=True) * (1.0 / width)
    spread = jnp.sum(centred * centred, axis=-1, keepdims=True) * (1.0 / width)
    scale = lax.rsqrt(spread + EPSILON)
    return centred * scale, scale


def gelu_parts(value):
    phi = 0.5 + 0.5 * lax.erf(value * 0.7071067811865476)
    bell = jnp.exp(value * value * -0.5)
    return value * phi, phi + value * bell * 0.3989422804014327


def feed_kernel(core, tok, cot, vectors, fcw, prw, *rest):
    ff, e2, dweights, dgain, dshift, dfcb, dbias, stamp, _, _ = rest[-10:]
    width, units = fcw.shape
    gain, shift = vectors[:, :width], vectors[:, width : 2 * width]
    step = pl.program_id(0)
    stamp[0] = core[0]
    xhat, _ = standardise(tok[...].astype(F32))
    normed = (xhat * gain + shift).astype(BF)
    hidden = mm(normed, fcw[...]) + vectors[:, 2 * width :]
    act, slope = gelu_parts(hidden)
    act = act.astype(BF)
    upstream = cot[...]
    ff[...] = mm(act, prw[...]).astype(BF)
    dhidden = (mm_nt(upstream, prw[...]) * slope).astype(BF)
    dnormed = mm_nt(dhidden, fcw[...])
    e2[...] = (dnormed * gain).astype(BF)

    @pl.when(step == 0)
    def _():
        for ref in (dweights, dgain, dshift, dfcb, dbias):
            ref[...] = jnp.zeros(ref.shape, F32)

    dweights[:units, :] += mm_tn(act, upstream)
    dweights[units:, :] += mm_tn(normed, dhidden)
    dgain[...] += fold(dnormed * xhat)
    dshift[...] += fold(dnormed)
    dfcb[...] += fold(dhidden.astype(F32))
    dbias[...] += fold(upstream.astype(F32))


def feed(core, tokens, cotangent, vectors, fcw, prw, first, count, tile, after=()):
    rows, width = tokens.shape
    units = fcw.shape[1]
    base = first // tile
    steps = count // tile
    source = pl.BlockSpec((tile, width), lambda i: (i + base, 0))
    target = pl.BlockSpec((tile, width), lambda i: (i, 0))

    def whole(*shape):
        return pl.BlockSpec(shape, lambda i: (0,) * len(shape))

    return pl.pallas_call(
        feed_kernel,
        grid=(steps,),
        in_specs=[
            pl.BlockSpec(memory_space=pltpu.SMEM),
            source,
            source,
            whole(1, 2 * width + units),
            whole(width, units),
            whole(units, width),
        ]
        + [pl.BlockSpec(memory_space=pl.ANY)] * len(after),
        out_specs=[
            target,
            target,
            whole(units + width, width),
            whole(8, width),
            whole(8, width),
            whole(8, units),
            whole(8, width),
            pl.BlockSpec(memory_space=pltpu.SMEM),
            pl.BlockSpec(memory_space=pl.ANY),
            pl.BlockSpec(memory_space=pl.ANY),
        ],
        out_shape=[
            jax.ShapeDtypeStruct((count, width), BF),
            jax.ShapeDtypeStruct((count, width), BF),
            jax.ShapeDtypeStruct((units + width, width), F32),
            jax.ShapeDtypeStruct((8, width), F32),
            jax.ShapeDtypeStruct((8, width), F32),
            jax.ShapeDtypeStruct((8, units), F32),
            jax.ShapeDtypeStruct((8, width), F32),
            jax.ShapeDtypeStruct((1,), jnp.int32),
            jax.ShapeDtypeStruct((rows, width), BF),
            jax.ShapeDtypeStruct((rows, width), F32),
        ],
        compiler_params=pltpu.CompilerParams(vmem_limit_bytes=VMEM_LIMIT),
        cost_estimate=pl.CostEstimate(flops=1, bytes_accessed=1, transcendentals=0),
        name="feed",
    )(core, tokens, cotangent, vectors, fcw, prw, *after)


def gate_kernel(passed, core, *refs):
    refs[-1][0] = core[0]


def gate(core, ready, passed):
    anywhere = pl.BlockSpec(memory_space=pl.ANY)
    scalar = pl.BlockSpec(memory_space=pltpu.SMEM)
    *handed, stamp = pl.pallas_call(
        functools.partial(gate_kernel, len(passed)),
        in_specs=[scalar] + [anywhere] * (len(passed) + len(ready)),
        out_specs=[anywhere] * len(passed) + [scalar],
        out_shape=[jax.ShapeDtypeStruct(a.shape, a.dtype) for a in passed]
        + [jax.ShapeDtypeStruct((1,), jnp.int32)],
        input_output_aliases={1 + k: k for k in range(len(passed))},
        cost_estimate=pl.CostEstimate(flops=1, bytes_accessed=1, transcendentals=0),
        name="gate",
    )(core, *passed, *ready)
    return handed, stamp[0]


def settle_kernel(core, mine, other, tokens, cotangent, shift, *refs):
    sent, out, grad = refs[-3:]
    total = mine[0].astype(F32) + other[0].astype(F32) + tokens[...].astype(F32) + shift[...]
    out[...] = total.astype(BF)
    sent[0] = total.astype(BF).astype(F32)
    total = mine[1].astype(F32) + other[1].astype(F32) + cotangent[...].astype(F32)
    grad[...] = total
    sent[1] = total


def settle(core, seq, mine, other, tokens, cotangent, shift, outs, after):
    _, half, width = mine.shape
    chunk = half // 2
    stacked = pl.BlockSpec((2, chunk, width), lambda i, core: (0, i, 0))
    rows = pl.BlockSpec((chunk, width), lambda i, core: ((seq * 2 + core[0]) * 2 + i, 0))
    anywhere = pl.BlockSpec(memory_space=pl.ANY)
    return pl.pallas_call(
        settle_kernel,
        grid_spec=pltpu.PrefetchScalarGridSpec(
            num_scalar_prefetch=1,
            grid=(2,),
            in_specs=[stacked, stacked, rows, rows]
            + [pl.BlockSpec((1, width), lambda i, core: (0, 0))]
            + [anywhere] * (2 + len(after)),
            out_specs=[stacked, rows, rows],
        ),
        out_shape=[jax.ShapeDtypeStruct(mine.shape, F32)]
        + [jax.ShapeDtypeStruct(a.shape, a.dtype) for a in outs],
        input_output_aliases={6: 1, 7: 2},
        cost_estimate=pl.CostEstimate(flops=1, bytes_accessed=1, transcendentals=0),
        name="settle",
    )(core, mine, other, tokens, cotangent, shift, *outs, *after)


def place_kernel(core, other, out_before, grad_before, out, grad):
    out[...] = other[0].astype(BF)
    grad[...] = other[1]


def place(core, seq, other, outs):
    _, half, width = other.shape
    chunk = half // 2
    rows = pl.BlockSpec((chunk, width), lambda i, core: ((seq * 2 + 1 - core[0]) * 2 + i, 0))
    return pl.pallas_call(
        place_kernel,
        grid_spec=pltpu.PrefetchScalarGridSpec(
            num_scalar_prefetch=1,
            grid=(2,),
            in_specs=[pl.BlockSpec((2, chunk, width), lambda i, core: (0, i, 0))]
            + [pl.BlockSpec(memory_space=pl.ANY)] * 2,
            out_specs=[rows, rows],
        ),
        out_shape=[jax.ShapeDtypeStruct(a.shape, a.dtype) for a in outs],
        input_output_aliases={2: 0, 3: 1},
        cost_estimate=pl.CostEstimate(flops=1, bytes_accessed=1, transcendentals=0),
        name="place",
    )(core, other, *outs)


def partner(array, lane):
    half = ROT // 2
    width = array.shape[-1]
    return jnp.where(
        lane < half,
        pltpu.roll(array, width - half, 1),
        pltpu.roll(array, half, 1),
    )


def attend_kernel(head, chunk, block, seq, pieces, more, final, waits, core, *refs):
    tok, cot, ff, e2, gain, shift, wqkv, bqkv, wdense, cosine, sine = refs[:11]
    carried = refs[11 : 11 + 4 * more]
    extra = refs[11 + 4 * more : 11 + 4 * (more + final)]
    waits += 4 * (more + final)
    tok_hbm, cot_hbm, ff_hbm, e2_hbm = tok, cot, ff, e2
    *refs, tok, cot, ff, e2, sum_s, part_s, in_sem, late_sem, out_sem = refs
    *give, keep, dweights, dgain, dshift, dbqkv, stamp = refs[11 + waits : 17 + waits + pieces]
    flat = refs[17 + waits + pieces]
    xhat_s, scale_s, n1_s, q_s, k_s, v_s, dc_s, ctx_s, dm_s, p_s, d_s, dqk_s = refs[17 + waits + pieces + final :]
    stamp[0] = core[0]
    length, width = tok.shape
    heads = q_s.shape[0]
    first = seq * length

    def fetch(i, k):
        rows = pl.ds(pl.multiple_of(i * chunk, chunk), chunk)
        there = pl.ds(pl.multiple_of(first + i * chunk, chunk), chunk)
        source, target = ((tok_hbm, tok), (cot_hbm, cot))[k]
        return pltpu.make_async_copy(source.at[there, :], target.at[rows, :], in_sem.at[i, k])

    for i in range(length // chunk):
        fetch(i, 0).start()
        fetch(i, 1).start()
    late = [
        pltpu.make_async_copy(ff_hbm.at[pl.ds(first, length), :], ff, late_sem.at[0]),
        pltpu.make_async_copy(e2_hbm.at[pl.ds(first, length), :], e2, late_sem.at[1]),
    ]
    if more:
        late.append(pltpu.make_async_copy(carried[0], sum_s, late_sem.at[2]))
    for copy in late:
        copy.start()

    triple = 3 * head
    half_rows = length // 2
    lane = lax.broadcasted_iota(jnp.int32, (chunk, 2 * head), 1) % head

    def before(i, carry):
        rows = pl.ds(pl.multiple_of(i * chunk, chunk), chunk)
        fetch(i, 0).wait()
        fetch(i, 1).wait()
        xhat, scale = standardise(tok[rows, :].astype(F32))
        xhat_s[rows, :] = xhat
        scale_s[rows, :] = scale
        normed = (xhat * gain[...] + shift[...]).astype(BF)
        n1_s[rows, :] = normed
        cos, sin = cosine[rows, :], sine[rows, :]
        dctx = mm_nt(cot[rows, :], wdense[...]).astype(BF)
        for h in range(heads):
            mixed = mm_nt(normed, wqkv[h * triple : (h + 1) * triple, :]) + bqkv[h : h + 1, :]
            turn = mixed[:, : 2 * head]
            turned = turn * cos + partner(turn, lane) * sin
            q_s[h, rows, :] = (turned[:, :head] * head**-0.5).astype(BF)
            k_s[h, rows, :] = turned[:, head:].astype(BF)
            v_s[h, rows, :] = mixed[:, 2 * head :].astype(BF)
            dc_s[h, rows, :] = dctx[:, h * head : (h + 1) * head]
        return carry

    lax.fori_loop(0, length // chunk, before, 0)

    causal = lax.broadcasted_iota(jnp.int32, (block, block), 1) <= lax.broadcasted_iota(
        jnp.int32, (block, block), 0
    )
    count = length // block

    def one_head(h, carry):
        for i in range(count):
            low, high = i * block, (i + 1) * block
            query = q_s[h, low:high, :]
            dctx = dc_s[h, low:high, :]
            pieces = [(low, high)] if i == 0 else [(0, low), (low, high)]
            scores = []
            for start, stop in pieces:
                part = mm_nt(query, k_s[h, start:stop, :])
                if start == low:
                    part = jnp.where(causal, part, MASKED)
                scores.append(part)
            top = functools.reduce(
                jnp.maximum, [jnp.max(part, axis=-1, keepdims=True) for part in scores]
            )
            scores = [jnp.exp(part - top) for part in scores]
            total = sum(jnp.sum(part, axis=-1, keepdims=True) for part in scores)
            inverse = 1.0 / total
            probs = [part * inverse for part in scores]
            context = 0.0
            for (start, stop), part in zip(pieces, probs):
                rounded = part.astype(BF)
                p_s[low:high, start:stop] = rounded
                context = context + mm(rounded, v_s[h, start:stop, :])
            ctx_s[h, low:high, :] = context.astype(BF)
            inner = jnp.sum(context * dctx.astype(F32), axis=-1, keepdims=True)
            dquery = 0.0
            for (start, stop), part in zip(pieces, probs):
                dprobs = mm_nt(dctx, v_s[h, start:stop, :])
                dscores = (part * (dprobs - inner)).astype(BF)
                d_s[low:high, start:stop] = dscores
                dquery = dquery + mm(dscores, k_s[h, start:stop, :])
            dqk_s[low:high, :head] = dquery * head**-0.5
        for j in range(count):
            low, high = j * block, (j + 1) * block
            dqk_s[low:high, head:] = mm_tn(q_s[h, low:, :], d_s[low:, low:high]).T
            dvalue = mm_tn(dc_s[h, low:, :], p_s[low:, low:high]).T
            dm_s[h, low:high, 2 * head :] = dvalue.astype(BF)
        for j in range(length // chunk):
            low, high = j * chunk, (j + 1) * chunk
            turn = dqk_s[low:high, :]
            back = turn * cosine[low:high, :] - partner(turn, lane) * sine[low:high, :]
            dm_s[h, low:high, : 2 * head] = back.astype(BF)
        return carry

    for h in range(heads):
        one_head(h, 0)

    late[0].wait()
    late[1].wait()
    for k, ref in enumerate((dgain, dshift, dbqkv)):
        ref[...] = carried[1 + k][...] if more else jnp.zeros(ref.shape, F32)

    def after(i, carry):
        rows = pl.ds(pl.multiple_of(i * chunk, chunk), chunk)
        context = jnp.concatenate([ctx_s[h, rows, :] for h in range(heads)], axis=-1)
        part = mm(context, wdense[...]) + ff[rows, :].astype(F32)
        dnormed = 0.0
        for h in range(heads):
            dmixed = dm_s[h, rows, :]
            dnormed = dnormed + mm(dmixed, wqkv[h * triple : (h + 1) * triple, :])
            dbqkv[h * 8 : (h + 1) * 8, :] += fold(dmixed.astype(F32))
        xhat, scale = xhat_s[rows, :], scale_s[rows, :]
        dgain[...] += fold(dnormed * xhat)
        dshift[...] += fold(dnormed)
        pulled = dnormed * gain[...] + e2[rows, :].astype(F32)
        mean = jnp.sum(pulled, axis=-1, keepdims=True) * (1.0 / width)
        along = jnp.sum(pulled * xhat, axis=-1, keepdims=True) * (1.0 / width)
        dinput = (scale * (pulled - mean - xhat * along)).astype(BF)
        side = (i * chunk) // half_rows
        there = pl.ds(pl.multiple_of(i * chunk - side * half_rows, chunk), chunk)

        part_s[0, rows, :] = part.astype(BF)
        part_s[1, rows, :] = dinput

        @pl.when(side == core[0])
        def _():
            for k in range(2):
                pltpu.make_async_copy(
                    part_s.at[k, rows, :], keep.at[k, there, :], out_sem.at[i, k]
                ).start()

        size = half_rows * 2 // pieces
        for j in range(pieces // 2):
            within = i * chunk - side * half_rows - j * size

            @pl.when((side != core[0]) & (within >= 0) & (within < size))
            def _():
                spot = pl.ds(pl.multiple_of(within, chunk), chunk)
                for k in range(2):
                    pltpu.make_async_copy(
                        part_s.at[k, rows, :],
                        give[k * (pieces // 2) + j].at[spot, :],
                        out_sem.at[i, k],
                    ).start()

        return carry

    lax.fori_loop(0, length // chunk, after, 0)
    if more:
        late[2].wait()
    for h in range(heads):
        rows = slice(h * triple, (h + 1) * triple)
        part = mm_tn(dm_s[h], n1_s[...])
        dweights[rows, :] = part + sum_s[rows, :] if more else part
        rows = slice(heads * triple + h * head, heads * triple + (h + 1) * head)
        part = mm_tn(ctx_s[h], cot[...])
        dweights[rows, :] = part + sum_s[rows, :] if more else part
    for i in range(length // chunk):
        for k in range(2):
            rows = slice(i * chunk, (i + 1) * chunk)
            pltpu.make_async_copy(
                part_s.at[k, rows, :], keep.at[k, pl.ds(0, chunk), :], out_sem.at[i, k]
            ).wait()
    if final:
        flat[...] = jnp.zeros(flat.shape, F32)
        for k, ref in enumerate((dgain, dshift, *extra)):
            flat[k : k + 1, : ref.shape[1]] = jnp.sum(ref[...], axis=0, keepdims=True)
        for h in range(heads):
            flat[6:7, h * triple : (h + 1) * triple] = jnp.sum(
                dbqkv[h * 8 : (h + 1) * 8, :], axis=0, keepdims=True
            )


def attend(
    core, tokens, cotangent, ff, e2, gain, shift, wqkv, bqkv, wdense, tables, seq, pieces, carried, extra, after
):
    width = tokens.shape[1]
    heads, triple = bqkv.shape
    head = triple // 3
    chunk, block = 256, 512
    half = LEN // 2
    lanes = max([width, heads * triple] + [vector.shape[1] for vector in extra])

    anywhere = pl.BlockSpec(memory_space=pl.ANY)

    def whole(*shape):
        return pl.BlockSpec(shape, lambda i: (0,) * len(shape))

    sums = [
        whole(4 * heads * head, width),
        whole(8, width),
        whole(8, width),
        whole(8 * heads, triple),
    ]
    return pl.pallas_call(
        functools.partial(attend_kernel, head, chunk, block, seq, pieces, bool(carried), bool(extra), len(after)),
        grid=(1,),
        in_specs=[
            pl.BlockSpec(memory_space=pltpu.SMEM),
            anywhere,
            anywhere,
            anywhere,
            anywhere,
            whole(1, width),
            whole(1, width),
            whole(heads * triple, width),
            whole(heads, triple),
            whole(heads * head, width),
            whole(LEN, 2 * head),
            whole(LEN, 2 * head),
        ]
        + ([anywhere, *sums[1:]] if carried else [])
        + [whole(*vector.shape) for vector in extra]
        + [pl.BlockSpec(memory_space=pl.ANY)] * len(after),
        out_specs=[
            *[anywhere] * pieces,
            anywhere,
            *sums,
            pl.BlockSpec(memory_space=pltpu.SMEM),
        ]
        + ([whole(8, lanes)] if extra else []),
        out_shape=[
            *[jax.ShapeDtypeStruct((2 * half // pieces, width), BF)] * pieces,
            jax.ShapeDtypeStruct((2, half, width), BF),
            jax.ShapeDtypeStruct((4 * heads * head, width), F32),
            jax.ShapeDtypeStruct((8, width), F32),
            jax.ShapeDtypeStruct((8, width), F32),
            jax.ShapeDtypeStruct((8 * heads, triple), F32),
            jax.ShapeDtypeStruct((1,), jnp.int32),
        ]
        + ([jax.ShapeDtypeStruct((8, lanes), F32)] if extra else []),
        scratch_shapes=[
            pltpu.VMEM((LEN, width), F32),
            pltpu.VMEM((LEN, 1), F32),
            pltpu.VMEM((LEN, width), BF),
            pltpu.VMEM((heads, LEN, head), BF),
            pltpu.VMEM((heads, LEN, head), BF),
            pltpu.VMEM((heads, LEN, head), BF),
            pltpu.VMEM((heads, LEN, head), BF),
            pltpu.VMEM((heads, LEN, head), BF),
            pltpu.VMEM((heads, LEN, triple), BF),
            pltpu.VMEM((LEN, LEN), BF),
            pltpu.VMEM((LEN, LEN), BF),
            pltpu.VMEM((LEN, 2 * head), F32),
            *[pltpu.VMEM((LEN, width), BF)] * 4,
            pltpu.VMEM((4 * heads * head, width), F32),
            pltpu.VMEM((2, LEN, width), BF),
            pltpu.SemaphoreType.DMA((LEN // chunk, 2)),
            pltpu.SemaphoreType.DMA((3,)),
            pltpu.SemaphoreType.DMA((LEN // chunk, 2)),
        ],
        compiler_params=pltpu.CompilerParams(vmem_limit_bytes=VMEM_LIMIT),
        cost_estimate=pl.CostEstimate(flops=1, bytes_accessed=1, transcendentals=0),
        name="attend",
    )(core, tokens, cotangent, ff, e2, gain, shift, wqkv, bqkv, wdense, *tables, *carried, *extra, *after)


def rotary_tables(head):
    half = ROT // 2
    position = np.arange(LEN, dtype=np.float32)
    inverse = (ROTARY_BASE ** (-(np.arange(half) * 2.0) / ROT)).astype(np.float32)
    angle = (position[:, None] * inverse[None, :]).astype(np.float64)
    cosine = np.ones((LEN, head), np.float32)
    sine = np.zeros((LEN, head), np.float32)
    cosine[:, :half] = cosine[:, half:ROT] = np.cos(angle)
    sine[:, :half] = -np.sin(angle)
    sine[:, half:ROT] = np.sin(angle)
    return np.tile(cosine, (1, 2)), np.tile(sine, (1, 2))


def swap(array, axis, bit):
    size = lax.axis_size(axis)
    return lax.ppermute(array, axis, [(i, i ^ bit) for i in range(size)])


def bits_of(size):
    return [1 << b for b in range(size.bit_length() - 1)]


def span(bits):
    masks = [0]
    for bit in bits:
        masks += [mask | bit for mask in masks]
    return masks


class Sum:
    def __init__(self, array, axis, groups, late):
        self.axis = axis
        self.stages = [(bits, True) for bits in groups]
        self.stages += [(bits, False) for bits in reversed(groups)]
        self.array = array
        self.received = []
        self.prepare(late)

    def place(self, bits, late):
        index = lax.axis_index(self.axis) + late
        return sum((((index & bit) != 0).astype(jnp.int32) << k) for k, bit in enumerate(bits))

    def prepare(self, late):
        if not self.stages:
            return
        bits, down = self.stages[0]
        if down:
            size = self.array.shape[0] >> len(bits)
            here = self.place(bits, late)
            self.sent = [
                lax.dynamic_slice_in_dim(self.array, (here ^ k) * size, size, 0).astype(BF)
                for k in range(1, 1 << len(bits))
            ]
        else:
            self.sent = [self.array.astype(BF)]

    def receive(self):
        bits, down = self.stages[0]
        masks = span(bits)[1:]
        sent = self.sent if down else self.sent * len(masks)
        self.received = [swap(part, self.axis, mask) for part, mask in zip(sent, masks)]
        return self.received

    def step(self, late):
        if not self.received:
            self.receive()
        bits, down = self.stages.pop(0)
        received, self.received = self.received, []
        here = self.place(bits, late)
        if down:
            size = self.array.shape[0] >> len(bits)
            total = lax.dynamic_slice_in_dim(self.array, here * size, size, 0)
            for part in received:
                total = total + part.astype(F32)
            self.array = total
        else:
            own = self.sent[0]
            parts = [own] + received
            pieces = []
            for k in range(len(parts)):
                piece = parts[k]
                for other in range(1, len(parts)):
                    piece = jnp.where(here == other, parts[k ^ other], piece)
                pieces.append(piece)
            self.array = jnp.concatenate(pieces, axis=0)
        self.prepare(late)

    def finish(self, late):
        while self.stages:
            self.step(late)
        return self.array.astype(F32)


def sum_doubling(array, axis):
    for bit in bits_of(lax.axis_size(axis)):
        array = array + swap(array, axis, bit)
    return array


def local(
    tokens,
    ln1_gain,
    ln1_bias,
    ln2_gain,
    ln2_bias,
    qkv_weight,
    qkv_bias,
    dense_weight,
    dense_bias,
    fc_weight,
    fc_bias,
    proj_weight,
    proj_bias,
    cotangent,
):
    rows, width = tokens.shape
    heads, triple = qkv_bias.shape
    units = fc_weight.shape[1]
    seqs = rows // LEN
    half = LEN // 2
    core = lax.axis_index("tensor") % 2
    dp_bits = bits_of(lax.axis_size("dp"))
    wqkv = qkv_weight.transpose(1, 2, 0).reshape(heads * triple, width)
    bqkv = qkv_bias.astype(F32)
    tables = rotary_tables(triple // 3)
    row = lambda vector: vector.astype(F32).reshape(1, -1)

    core_ref = core.reshape(1).astype(jnp.int32)

    def attend_rows(s, carried, after):
        extra = (dgain2, dshift2, dfcb, dbias) if s == seqs - 1 else ()
        results = attend(
            core_ref,
            tokens,
            cotangent,
            ff,
            e2,
            row(ln1_gain),
            row(ln1_bias),
            wqkv,
            bqkv,
            dense_weight,
            tables,
            s,
            4 if s < seqs - 1 else 2,
            carried,
            extra,
            after,
        )
        *results, flat = results if extra else (*results, None)
        *give, keep, a, b, c, d, stamp = results
        return give, keep, (a, b, c, d), stamp[0], flat

    def cross(give, keep):
        others = [swap(piece, "tensor", 1) for piece in give]
        n = len(give) // 2
        return jnp.stack(
            [
                (keep[k].astype(F32) + jnp.concatenate(others[n * k : n * (k + 1)]).astype(F32)).astype(BF)
                for k in range(2)
            ]
        )

    shift = row(dense_bias) + row(proj_bias)

    groups = [(dp_bits[0],), tuple(dp_bits[1:3])] + [(bit,) for bit in dp_bits[3:]]
    ff, e2, dfeed, dgain2, dshift2, dfcb, dbias, stamp, *outs = feed(
        core_ref,
        tokens,
        cotangent,
        row(jnp.concatenate([ln2_gain, ln2_bias, fc_bias])),
        fc_weight,
        proj_weight,
        0,
        rows,
        1024,
    )
    now = stamp[0]
    work = Sum(dfeed, "dp", groups, now - core)
    mine, sent, carried = [], [], ()
    after = tuple(work.sent)

    def settle_rows(s, other, after):
        packet, *into = settle(
            core_ref, s, mine[s], other, tokens, cotangent, shift, outs, after
        )
        return packet, into

    pending = []
    bits = list(dp_bits)
    for s in range(seqs):
        give, keep, carried, now, flat = attend_rows(s, carried, after)
        if s < seqs - 1:
            work.step(now - core)
            ready = list(work.sent)
        else:
            ready = list(work.receive())
            packed = Sum(carried[0], "dp", groups, now - core)
            ready += packed.sent
        give, _ = gate(core_ref, ready, give)
        if s >= 1:
            other = swap(mine[s - 1], "tensor", 2)
            (keep,), now = gate(core_ref, [other], [keep])
        mine.append(cross(give, keep))
        if s == seqs - 1:
            for bit in bits[1:2]:
                flat = flat + swap(flat, "dp", bit)
            (flat,), stamp = gate(core_ref, [mine[s]], [flat])
            for bit in bits[2:]:
                flat = flat + swap(flat, "dp", bit)
            packed.step(stamp - core)
            work.step(stamp - core)
        after = (mine[s], *work.sent)
        if s >= 1:
            pending.append(other)

    (flat,), stamp = gate(core_ref, packed.sent, [flat])
    flat = flat + swap(flat, "dp", bits[0])
    work.sent, _ = gate(core_ref, [flat], work.sent)
    for s, other in enumerate(pending):
        packet, outs = settle_rows(s, other, tuple(packed.sent))
        sent.append(packet)
    _, stamp = gate(core_ref, [sent[-1]] if sent else [], [])
    if packed.stages:
        packed.step(stamp - core)
    if packed.stages:
        packed.step(stamp - core)
    other = swap(mine[-1], "tensor", 2)
    _, stamp = gate(core_ref, [other], [])
    both = work.finish(stamp - core)
    dproj, dfc = both[:units], both[units:]
    packet, outs = settle_rows(seqs - 1, other, (*packed.sent, dproj, dfc))
    (flat, *last), stamp = gate(core_ref, [packet], [flat, *sent])
    for s, each in enumerate(last):
        outs = place(core_ref, s, swap(each, "tensor", 1), outs)
    if packed.stages:
        packed.received, stamp = gate(core_ref, outs, packed.receive())
    norms = flat[:4, :width]
    norms = norms + swap(norms, "tensor", 1)
    norms = norms + swap(norms, "tensor", 2)
    outs = place(core_ref, seqs - 1, swap(packet, "tensor", 1), outs)
    block_out, input_grad = outs
    packed = packed.finish(stamp - core)
    dqkv = packed[: heads * triple].reshape(heads, triple, width).transpose(2, 0, 1)
    ddense = packed[heads * triple :]

    dfcb, dbias, dbqkv = flat[4, :units], flat[5, :width], flat[6, : heads * triple]
    return (
        block_out,
        input_grad,
        norms[0],
        norms[1],
        norms[2],
        norms[3],
        dqkv,
        dbqkv.reshape(heads, triple),
        ddense,
        dbias,
        dfc,
        dfcb,
        dproj,
        dbias,
    )


def solution(mesh):
    in_specs = (
        P("dp", None),
        P(),
        P(),
        P(),
        P(),
        P(None, "tensor", None),
        P("tensor", None),
        P("tensor", None),
        P(),
        P(None, "tensor"),
        P("tensor"),
        P("tensor", None),
        P(),
        P("dp", None),
    )
    out_specs = (
        P("dp", None),
        P("dp", None),
        P(),
        P(),
        P(),
        P(),
        P(None, "tensor", None),
        P("tensor", None),
        P("tensor", None),
        P(),
        P(None, "tensor"),
        P("tensor"),
        P("tensor", None),
        P(),
    )
    return jax.shard_map(local, mesh=mesh, in_specs=in_specs, out_specs=out_specs, check_vma=False)
```

```python
import functools

import jax
import jax.numpy as jnp
import numpy as np
from jax import lax
from jax.experimental import pallas as pl
from jax.experimental.pallas import tpu as pltpu
from jax.sharding import PartitionSpec as P

ROT = 16
LEN = 1024
EPSILON = 1e-05
ROTARY_BASE = 10000.0
MASKED = -1e30
VMEM_LIMIT = 56 * 1024 * 1024
BF = jnp.bfloat16
F32 = jnp.float32


def mm(a, b):
    return lax.dot_general(a, b, (((1,), (0,)), ((), ())), preferred_element_type=F32)


def mm_nt(a, b):
    return lax.dot_general(a, b, (((1,), (1,)), ((), ())), preferred_element_type=F32)


def mm_tn(a, b):
    return lax.dot_general(a, b, (((0,), (0,)), ((), ())), preferred_element_type=F32)


def fold(array):
    rows, width = array.shape
    return jnp.sum(array.reshape(rows // 8, 8, width), axis=0)


def standardise(rows):
    width = rows.shape[-1]
    centred = rows - jnp.sum(rows, axis=-1, keepdims=True) * (1.0 / width)
    spread = jnp.sum(centred * centred, axis=-1, keepdims=True) * (1.0 / width)
    scale = lax.rsqrt(spread + EPSILON)
    return centred * scale, scale


def gelu_parts(value):
    phi = 0.5 + 0.5 * lax.erf(value * 0.7071067811865476)
    bell = jnp.exp(value * value * -0.5)
    return value * phi, phi + value * bell * 0.3989422804014327


def feed_kernel(core, tok, cot, vectors, fcw, prw, *rest):
    ff, e2, dweights, dgain, dshift, dfcb, dbias, stamp, _, _ = rest[-10:]
    width, units = fcw.shape
    gain, shift = vectors[:, :width], vectors[:, width : 2 * width]
    step = pl.program_id(0)
    stamp[0] = core[0]
    xhat, _ = standardise(tok[...].astype(F32))
    normed = (xhat * gain + shift).astype(BF)
    hidden = mm(normed, fcw[...]) + vectors[:, 2 * width :]
    act, slope = gelu_parts(hidden)
    act = act.astype(BF)
    upstream = cot[...]
    ff[...] = mm(act, prw[...]).astype(BF)
    dhidden = (mm_nt(upstream, prw[...]) * slope).astype(BF)
    dnormed = mm_nt(dhidden, fcw[...])
    e2[...] = (dnormed * gain).astype(BF)

    @pl.when(step == 0)
    def _():
        for ref in (dweights, dgain, dshift, dfcb, dbias):
            ref[...] = jnp.zeros(ref.shape, F32)

    dweights[:units, :] += mm_tn(act, upstream)
    dweights[units:, :] += mm_tn(normed, dhidden)
    dgain[...] += fold(dnormed * xhat)
    dshift[...] += fold(dnormed)
    dfcb[...] += fold(dhidden.astype(F32))
    dbias[...] += fold(upstream.astype(F32))


def feed(core, tokens, cotangent, vectors, fcw, prw, first, count, tile, after=()):
    rows, width = tokens.shape
    units = fcw.shape[1]
    base = first // tile
    steps = count // tile
    source = pl.BlockSpec((tile, width), lambda i: (i + base, 0))
    target = pl.BlockSpec((tile, width), lambda i: (i, 0))

    def whole(*shape):
        return pl.BlockSpec(shape, lambda i: (0,) * len(shape))

    return pl.pallas_call(
        feed_kernel,
        grid=(steps,),
        in_specs=[
            pl.BlockSpec(memory_space=pltpu.SMEM),
            source,
            source,
            whole(1, 2 * width + units),
            whole(width, units),
            whole(units, width),
        ]
        + [pl.BlockSpec(memory_space=pl.ANY)] * len(after),
        out_specs=[
            target,
            target,
            whole(units + width, width),
            whole(8, width),
            whole(8, width),
            whole(8, units),
            whole(8, width),
            pl.BlockSpec(memory_space=pltpu.SMEM),
            pl.BlockSpec(memory_space=pl.ANY),
            pl.BlockSpec(memory_space=pl.ANY),
        ],
        out_shape=[
            jax.ShapeDtypeStruct((count, width), BF),
            jax.ShapeDtypeStruct((count, width), BF),
            jax.ShapeDtypeStruct((units + width, width), F32),
            jax.ShapeDtypeStruct((8, width), F32),
            jax.ShapeDtypeStruct((8, width), F32),
            jax.ShapeDtypeStruct((8, units), F32),
            jax.ShapeDtypeStruct((8, width), F32),
            jax.ShapeDtypeStruct((1,), jnp.int32),
            jax.ShapeDtypeStruct((rows, width), BF),
            jax.ShapeDtypeStruct((rows, width), F32),
        ],
        compiler_params=pltpu.CompilerParams(vmem_limit_bytes=VMEM_LIMIT),
        cost_estimate=pl.CostEstimate(flops=1, bytes_accessed=1, transcendentals=0),
        name="feed",
    )(core, tokens, cotangent, vectors, fcw, prw, *after)


def gate_kernel(passed, core, *refs):
    refs[-1][0] = core[0]


def gate(core, ready, passed):
    anywhere = pl.BlockSpec(memory_space=pl.ANY)
    scalar = pl.BlockSpec(memory_space=pltpu.SMEM)
    *handed, stamp = pl.pallas_call(
        functools.partial(gate_kernel, len(passed)),
        in_specs=[scalar] + [anywhere] * (len(passed) + len(ready)),
        out_specs=[anywhere] * len(passed) + [scalar],
        out_shape=[jax.ShapeDtypeStruct(a.shape, a.dtype) for a in passed]
        + [jax.ShapeDtypeStruct((1,), jnp.int32)],
        input_output_aliases={1 + k: k for k in range(len(passed))},
        cost_estimate=pl.CostEstimate(flops=1, bytes_accessed=1, transcendentals=0),
        name="gate",
    )(core, *passed, *ready)
    return handed, stamp[0]


def settle_kernel(core, mine, other, tokens, cotangent, shift, *refs):
    sent, out, grad = refs[-3:]
    total = mine[0].astype(F32) + other[0].astype(F32) + tokens[...].astype(F32) + shift[...]
    out[...] = total.astype(BF)
    sent[0] = total.astype(BF).astype(F32)
    total = mine[1].astype(F32) + other[1].astype(F32) + cotangent[...].astype(F32)
    grad[...] = total
    sent[1] = total


def settle(core, seq, mine, other, tokens, cotangent, shift, outs, after):
    _, half, width = mine.shape
    chunk = half // 2
    stacked = pl.BlockSpec((2, chunk, width), lambda i, core: (0, i, 0))
    rows = pl.BlockSpec((chunk, width), lambda i, core: ((seq * 2 + core[0]) * 2 + i, 0))
    anywhere = pl.BlockSpec(memory_space=pl.ANY)
    return pl.pallas_call(
        settle_kernel,
        grid_spec=pltpu.PrefetchScalarGridSpec(
            num_scalar_prefetch=1,
            grid=(2,),
            in_specs=[stacked, stacked, rows, rows]
            + [pl.BlockSpec((1, width), lambda i, core: (0, 0))]
            + [anywhere] * (2 + len(after)),
            out_specs=[stacked, rows, rows],
        ),
        out_shape=[jax.ShapeDtypeStruct(mine.shape, F32)]
        + [jax.ShapeDtypeStruct(a.shape, a.dtype) for a in outs],
        input_output_aliases={6: 1, 7: 2},
        cost_estimate=pl.CostEstimate(flops=1, bytes_accessed=1, transcendentals=0),
        name="settle",
    )(core, mine, other, tokens, cotangent, shift, *outs, *after)


def place_kernel(core, other, out_before, grad_before, out, grad):
    out[...] = other[0].astype(BF)
    grad[...] = other[1]


def place(core, seq, other, outs):
    _, half, width = other.shape
    chunk = half // 2
    rows = pl.BlockSpec((chunk, width), lambda i, core: ((seq * 2 + 1 - core[0]) * 2 + i, 0))
    return pl.pallas_call(
        place_kernel,
        grid_spec=pltpu.PrefetchScalarGridSpec(
            num_scalar_prefetch=1,
            grid=(2,),
            in_specs=[pl.BlockSpec((2, chunk, width), lambda i, core: (0, i, 0))]
            + [pl.BlockSpec(memory_space=pl.ANY)] * 2,
            out_specs=[rows, rows],
        ),
        out_shape=[jax.ShapeDtypeStruct(a.shape, a.dtype) for a in outs],
        input_output_aliases={2: 0, 3: 1},
        cost_estimate=pl.CostEstimate(flops=1, bytes_accessed=1, transcendentals=0),
        name="place",
    )(core, other, *outs)


def partner(array, lane):
    half = ROT // 2
    width = array.shape[-1]
    return jnp.where(
        lane < half,
        pltpu.roll(array, width - half, 1),
        pltpu.roll(array, half, 1),
    )


def attend_kernel(head, chunk, block, seq, pieces, more, final, waits, core, *refs):
    tok, cot, ff, e2, gain, shift, wqkv, bqkv, wdense, cosine, sine = refs[:11]
    carried = refs[11 : 11 + 4 * more]
    extra = refs[11 + 4 * more : 11 + 4 * (more + final)]
    waits += 4 * (more + final)
    tok_hbm, cot_hbm, ff_hbm, e2_hbm = tok, cot, ff, e2
    *refs, tok, cot, ff, e2, sum_s, part_s, in_sem, late_sem, out_sem = refs
    *give, keep, dweights, dgain, dshift, dbqkv, stamp = refs[11 + waits : 17 + waits + pieces]
    flat = refs[17 + waits + pieces]
    xhat_s, scale_s, n1_s, q_s, k_s, v_s, dc_s, ctx_s, dm_s, p_s, d_s, dqk_s = refs[17 + waits + pieces + final :]
    stamp[0] = core[0]
    length, width = tok.shape
    heads = q_s.shape[0]
    first = seq * length

    def fetch(i, k):
        rows = pl.ds(pl.multiple_of(i * chunk, chunk), chunk)
        there = pl.ds(pl.multiple_of(first + i * chunk, chunk), chunk)
        source, target = ((tok_hbm, tok), (cot_hbm, cot))[k]
        return pltpu.make_async_copy(source.at[there, :], target.at[rows, :], in_sem.at[i, k])

    for i in range(length // chunk):
        fetch(i, 0).start()
        fetch(i, 1).start()
    late = [
        pltpu.make_async_copy(ff_hbm.at[pl.ds(first, length), :], ff, late_sem.at[0]),
        pltpu.make_async_copy(e2_hbm.at[pl.ds(first, length), :], e2, late_sem.at[1]),
    ]
    if more:
        late.append(pltpu.make_async_copy(carried[0], sum_s, late_sem.at[2]))
    for copy in late:
        copy.start()

    triple = 3 * head
    half_rows = length // 2
    lane = lax.broadcasted_iota(jnp.int32, (chunk, 2 * head), 1) % head

    def before(i, carry):
        rows = pl.ds(pl.multiple_of(i * chunk, chunk), chunk)
        fetch(i, 0).wait()
        fetch(i, 1).wait()
        xhat, scale = standardise(tok[rows, :].astype(F32))
        xhat_s[rows, :] = xhat
        scale_s[rows, :] = scale
        normed = (xhat * gain[...] + shift[...]).astype(BF)
        n1_s[rows, :] = normed
        cos, sin = cosine[rows, :], sine[rows, :]
        dctx = mm_nt(cot[rows, :], wdense[...]).astype(BF)
        for h in range(heads):
            mixed = mm_nt(normed, wqkv[h * triple : (h + 1) * triple, :]) + bqkv[h : h + 1, :]
            turn = mixed[:, : 2 * head]
            turned = turn * cos + partner(turn, lane) * sin
            q_s[h, rows, :] = (turned[:, :head] * head**-0.5).astype(BF)
            k_s[h, rows, :] = turned[:, head:].astype(BF)
            v_s[h, rows, :] = mixed[:, 2 * head :].astype(BF)
            dc_s[h, rows, :] = dctx[:, h * head : (h + 1) * head]
        return carry

    lax.fori_loop(0, length // chunk, before, 0)

    causal = lax.broadcasted_iota(jnp.int32, (block, block), 1) <= lax.broadcasted_iota(
        jnp.int32, (block, block), 0
    )
    count = length // block

    def one_head(h, carry):
        for i in range(count):
            low, high = i * block, (i + 1) * block
            query = q_s[h, low:high, :]
            dctx = dc_s[h, low:high, :]
            pieces = [(low, high)] if i == 0 else [(0, low), (low, high)]
            scores = []
            for start, stop in pieces:
                part = mm_nt(query, k_s[h, start:stop, :])
                if start == low:
                    part = jnp.where(causal, part, MASKED)
                scores.append(part)
            top = functools.reduce(
                jnp.maximum, [jnp.max(part, axis=-1, keepdims=True) for part in scores]
            )
            scores = [jnp.exp(part - top) for part in scores]
            total = sum(jnp.sum(part, axis=-1, keepdims=True) for part in scores)
            inverse = 1.0 / total
            probs = [part * inverse for part in scores]
            context = 0.0
            for (start, stop), part in zip(pieces, probs):
                rounded = part.astype(BF)
                p_s[low:high, start:stop] = rounded
                context = context + mm(rounded, v_s[h, start:stop, :])
            ctx_s[h, low:high, :] = context.astype(BF)
            inner = jnp.sum(context * dctx.astype(F32), axis=-1, keepdims=True)
            dquery = 0.0
            for (start, stop), part in zip(pieces, probs):
                dprobs = mm_nt(dctx, v_s[h, start:stop, :])
                dscores = (part * (dprobs - inner)).astype(BF)
                d_s[low:high, start:stop] = dscores
                dquery = dquery + mm(dscores, k_s[h, start:stop, :])
            dqk_s[low:high, :head] = dquery * head**-0.5
        for j in range(count):
            low, high = j * block, (j + 1) * block
            dqk_s[low:high, head:] = mm_tn(q_s[h, low:, :], d_s[low:, low:high]).T
            dvalue = mm_tn(dc_s[h, low:, :], p_s[low:, low:high]).T
            dm_s[h, low:high, 2 * head :] = dvalue.astype(BF)
        for j in range(length // chunk):
            low, high = j * chunk, (j + 1) * chunk
            turn = dqk_s[low:high, :]
            back = turn * cosine[low:high, :] - partner(turn, lane) * sine[low:high, :]
            dm_s[h, low:high, : 2 * head] = back.astype(BF)
        return carry

    for h in range(heads):
        one_head(h, 0)

    late[0].wait()
    late[1].wait()
    for k, ref in enumerate((dgain, dshift, dbqkv)):
        ref[...] = carried[1 + k][...] if more else jnp.zeros(ref.shape, F32)

    def after(i, carry):
        rows = pl.ds(pl.multiple_of(i * chunk, chunk), chunk)
        context = jnp.concatenate([ctx_s[h, rows, :] for h in range(heads)], axis=-1)
        part = mm(context, wdense[...]) + ff[rows, :].astype(F32)
        dnormed = 0.0
        for h in range(heads):
            dmixed = dm_s[h, rows, :]
            dnormed = dnormed + mm(dmixed, wqkv[h * triple : (h + 1) * triple, :])
            dbqkv[h * 8 : (h + 1) * 8, :] += fold(dmixed.astype(F32))
        xhat, scale = xhat_s[rows, :], scale_s[rows, :]
        dgain[...] += fold(dnormed * xhat)
        dshift[...] += fold(dnormed)
        pulled = dnormed * gain[...] + e2[rows, :].astype(F32)
        mean = jnp.sum(pulled, axis=-1, keepdims=True) * (1.0 / width)
        along = jnp.sum(pulled * xhat, axis=-1, keepdims=True) * (1.0 / width)
        dinput = (scale * (pulled - mean - xhat * along)).astype(BF)
        side = (i * chunk) // half_rows
        there = pl.ds(pl.multiple_of(i * chunk - side * half_rows, chunk), chunk)

        part_s[0, rows, :] = part.astype(BF)
        part_s[1, rows, :] = dinput

        @pl.when(side == core[0])
        def _():
            for k in range(2):
                pltpu.make_async_copy(
                    part_s.at[k, rows, :], keep.at[k, there, :], out_sem.at[i, k]
                ).start()

        size = half_rows * 2 // pieces
        for j in range(pieces // 2):
            within = i * chunk - side * half_rows - j * size

            @pl.when((side != core[0]) & (within >= 0) & (within < size))
            def _():
                spot = pl.ds(pl.multiple_of(within, chunk), chunk)
                for k in range(2):
                    pltpu.make_async_copy(
                        part_s.at[k, rows, :],
                        give[k * (pieces // 2) + j].at[spot, :],
                        out_sem.at[i, k],
                    ).start()

        return carry

    lax.fori_loop(0, length // chunk, after, 0)
    if more:
        late[2].wait()
    for h in range(heads):
        rows = slice(h * triple, (h + 1) * triple)
        part = mm_tn(dm_s[h], n1_s[...])
        dweights[rows, :] = part + sum_s[rows, :] if more else part
        rows = slice(heads * triple + h * head, heads * triple + (h + 1) * head)
        part = mm_tn(ctx_s[h], cot[...])
        dweights[rows, :] = part + sum_s[rows, :] if more else part
    for i in range(length // chunk):
        for k in range(2):
            rows = slice(i * chunk, (i + 1) * chunk)
            pltpu.make_async_copy(
                part_s.at[k, rows, :], keep.at[k, pl.ds(0, chunk), :], out_sem.at[i, k]
            ).wait()
    if final:
        flat[...] = jnp.zeros(flat.shape, F32)
        for k, ref in enumerate((dgain, dshift, *extra)):
            flat[k : k + 1, : ref.shape[1]] = jnp.sum(ref[...], axis=0, keepdims=True)
        for h in range(heads):
            flat[6:7, h * triple : (h + 1) * triple] = jnp.sum(
                dbqkv[h * 8 : (h + 1) * 8, :], axis=0, keepdims=True
            )


def attend(
    core, tokens, cotangent, ff, e2, gain, shift, wqkv, bqkv, wdense, tables, seq, pieces, carried, extra, after
):
    width = tokens.shape[1]
    heads, triple = bqkv.shape
    head = triple // 3
    chunk, block = 256, 512
    half = LEN // 2
    lanes = max([width, heads * triple] + [vector.shape[1] for vector in extra])

    anywhere = pl.BlockSpec(memory_space=pl.ANY)

    def whole(*shape):
        return pl.BlockSpec(shape, lambda i: (0,) * len(shape))

    sums = [
        whole(4 * heads * head, width),
        whole(8, width),
        whole(8, width),
        whole(8 * heads, triple),
    ]
    return pl.pallas_call(
        functools.partial(attend_kernel, head, chunk, block, seq, pieces, bool(carried), bool(extra), len(after)),
        grid=(1,),
        in_specs=[
            pl.BlockSpec(memory_space=pltpu.SMEM),
            anywhere,
            anywhere,
            anywhere,
            anywhere,
            whole(1, width),
            whole(1, width),
            whole(heads * triple, width),
            whole(heads, triple),
            whole(heads * head, width),
            whole(LEN, 2 * head),
            whole(LEN, 2 * head),
        ]
        + ([anywhere, *sums[1:]] if carried else [])
        + [whole(*vector.shape) for vector in extra]
        + [pl.BlockSpec(memory_space=pl.ANY)] * len(after),
        out_specs=[
            *[anywhere] * pieces,
            anywhere,
            *sums,
            pl.BlockSpec(memory_space=pltpu.SMEM),
        ]
        + ([whole(8, lanes)] if extra else []),
        out_shape=[
            *[jax.ShapeDtypeStruct((2 * half // pieces, width), BF)] * pieces,
            jax.ShapeDtypeStruct((2, half, width), BF),
            jax.ShapeDtypeStruct((4 * heads * head, width), F32),
            jax.ShapeDtypeStruct((8, width), F32),
            jax.ShapeDtypeStruct((8, width), F32),
            jax.ShapeDtypeStruct((8 * heads, triple), F32),
            jax.ShapeDtypeStruct((1,), jnp.int32),
        ]
        + ([jax.ShapeDtypeStruct((8, lanes), F32)] if extra else []),
        scratch_shapes=[
            pltpu.VMEM((LEN, width), F32),
            pltpu.VMEM((LEN, 1), F32),
            pltpu.VMEM((LEN, width), BF),
            pltpu.VMEM((heads, LEN, head), BF),
            pltpu.VMEM((heads, LEN, head), BF),
            pltpu.VMEM((heads, LEN, head), BF),
            pltpu.VMEM((heads, LEN, head), BF),
            pltpu.VMEM((heads, LEN, head), BF),
            pltpu.VMEM((heads, LEN, triple), BF),
            pltpu.VMEM((LEN, LEN), BF),
            pltpu.VMEM((LEN, LEN), BF),
            pltpu.VMEM((LEN, 2 * head), F32),
            *[pltpu.VMEM((LEN, width), BF)] * 4,
            pltpu.VMEM((4 * heads * head, width), F32),
            pltpu.VMEM((2, LEN, width), BF),
            pltpu.SemaphoreType.DMA((LEN // chunk, 2)),
            pltpu.SemaphoreType.DMA((3,)),
            pltpu.SemaphoreType.DMA((LEN // chunk, 2)),
        ],
        compiler_params=pltpu.CompilerParams(vmem_limit_bytes=VMEM_LIMIT),
        cost_estimate=pl.CostEstimate(flops=1, bytes_accessed=1, transcendentals=0),
        name="attend",
    )(core, tokens, cotangent, ff, e2, gain, shift, wqkv, bqkv, wdense, *tables, *carried, *extra, *after)


def rotary_tables(head):
    half = ROT // 2
    position = np.arange(LEN, dtype=np.float32)
    inverse = (ROTARY_BASE ** (-(np.arange(half) * 2.0) / ROT)).astype(np.float32)
    angle = (position[:, None] * inverse[None, :]).astype(np.float64)
    cosine = np.ones((LEN, head), np.float32)
    sine = np.zeros((LEN, head), np.float32)
    cosine[:, :half] = cosine[:, half:ROT] = np.cos(angle)
    sine[:, :half] = -np.sin(angle)
    sine[:, half:ROT] = np.sin(angle)
    return np.tile(cosine, (1, 2)), np.tile(sine, (1, 2))


def swap(array, axis, bit):
    size = lax.axis_size(axis)
    return lax.ppermute(array, axis, [(i, i ^ bit) for i in range(size)])


def bits_of(size):
    return [1 << b for b in range(size.bit_length() - 1)]


def span(bits):
    masks = [0]
    for bit in bits:
        masks += [mask | bit for mask in masks]
    return masks


class Sum:
    def __init__(self, array, axis, groups, late):
        self.axis = axis
        self.stages = [(bits, True) for bits in groups]
        self.stages += [(bits, False) for bits in reversed(groups)]
        self.array = array
        self.received = []
        self.prepare(late)

    def place(self, bits, late):
        index = lax.axis_index(self.axis) + late
        return sum((((index & bit) != 0).astype(jnp.int32) << k) for k, bit in enumerate(bits))

    def prepare(self, late):
        if not self.stages:
            return
        bits, down = self.stages[0]
        if down:
            size = self.array.shape[0] >> len(bits)
            here = self.place(bits, late)
            self.sent = [
                lax.dynamic_slice_in_dim(self.array, (here ^ k) * size, size, 0).astype(BF)
                for k in range(1, 1 << len(bits))
            ]
        else:
            self.sent = [self.array.astype(BF)]

    def receive(self):
        bits, down = self.stages[0]
        masks = span(bits)[1:]
        sent = self.sent if down else self.sent * len(masks)
        self.received = [swap(part, self.axis, mask) for part, mask in zip(sent, masks)]
        return self.received

    def step(self, late):
        if not self.received:
            self.receive()
        bits, down = self.stages.pop(0)
        received, self.received = self.received, []
        here = self.place(bits, late)
        if down:
            size = self.array.shape[0] >> len(bits)
            total = lax.dynamic_slice_in_dim(self.array, here * size, size, 0)
            for part in received:
                total = total + part.astype(F32)
            self.array = total
        else:
            own = self.sent[0]
            parts = [own] + received
            pieces = []
            for k in range(len(parts)):
                piece = parts[k]
                for other in range(1, len(parts)):
                    piece = jnp.where(here == other, parts[k ^ other], piece)
                pieces.append(piece)
            self.array = jnp.concatenate(pieces, axis=0)
        self.prepare(late)

    def finish(self, late):
        while self.stages:
            self.step(late)
        return self.array.astype(F32)


def sum_doubling(array, axis):
    for bit in bits_of(lax.axis_size(axis)):
        array = array + swap(array, axis, bit)
    return array


def local(
    tokens,
    ln1_gain,
    ln1_bias,
    ln2_gain,
    ln2_bias,
    qkv_weight,
    qkv_bias,
    dense_weight,
    dense_bias,
    fc_weight,
    fc_bias,
    proj_weight,
    proj_bias,
    cotangent,
):
    rows, width = tokens.shape
    heads, triple = qkv_bias.shape
    units = fc_weight.shape[1]
    seqs = rows // LEN
    half = LEN // 2
    core = lax.axis_index("tensor") % 2
    dp_bits = bits_of(lax.axis_size("dp"))
    wqkv = qkv_weight.transpose(1, 2, 0).reshape(heads * triple, width)
    bqkv = qkv_bias.astype(F32)
    tables = rotary_tables(triple // 3)
    row = lambda vector: vector.astype(F32).reshape(1, -1)

    core_ref = core.reshape(1).astype(jnp.int32)

    def attend_rows(s, carried, after):
        extra = (dgain2, dshift2, dfcb, dbias) if s == seqs - 1 else ()
        results = attend(
            core_ref,
            tokens,
            cotangent,
            ff,
            e2,
            row(ln1_gain),
            row(ln1_bias),
            wqkv,
            bqkv,
            dense_weight,
            tables,
            s,
            4 if s < seqs - 1 else 2,
            carried,
            extra,
            after,
        )
        *results, flat = results if extra else (*results, None)
        *give, keep, a, b, c, d, stamp = results
        return give, keep, (a, b, c, d), stamp[0], flat

    def cross(give, keep):
        others = [swap(piece, "tensor", 1) for piece in give]
        n = len(give) // 2
        return jnp.stack(
            [
                (keep[k].astype(F32) + jnp.concatenate(others[n * k : n * (k + 1)]).astype(F32)).astype(BF)
                for k in range(2)
            ]
        )

    shift = row(dense_bias) + row(proj_bias)

    groups = [(dp_bits[0],), tuple(dp_bits[1:3])] + [(bit,) for bit in dp_bits[3:]]
    ff, e2, dfeed, dgain2, dshift2, dfcb, dbias, stamp, *outs = feed(
        core_ref,
        tokens,
        cotangent,
        row(jnp.concatenate([ln2_gain, ln2_bias, fc_bias])),
        fc_weight,
        proj_weight,
        0,
        rows,
        1024,
    )
    now = stamp[0]
    work = Sum(dfeed, "dp", groups, now - core)
    mine, sent, carried = [], [], ()
    after = tuple(work.sent)

    def settle_rows(s, other, after):
        packet, *into = settle(
            core_ref, s, mine[s], other, tokens, cotangent, shift, outs, after
        )
        return packet, into

    pending = []
    bits = list(dp_bits)
    for s in range(seqs):
        give, keep, carried, now, flat = attend_rows(s, carried, after)
        if s < seqs - 1:
            work.step(now - core)
            ready = list(work.sent)
        else:
            ready = list(work.receive())
            packed = Sum(carried[0], "dp", groups, now - core)
            ready += packed.sent
        give, _ = gate(core_ref, ready, give)
        if s >= 1:
            other = swap(mine[s - 1], "tensor", 2)
            (keep,), now = gate(core_ref, [other], [keep])
        mine.append(cross(give, keep))
        if s == seqs - 1:
            for bit in bits[1:2]:
                flat = flat + swap(flat, "dp", bit)
            (flat,), stamp = gate(core_ref, [mine[s]], [flat])
            for bit in bits[2:]:
                flat = flat + swap(flat, "dp", bit)
            packed.step(stamp - core)
            work.step(stamp - core)
        after = (mine[s], *work.sent)
        if s >= 1:
            pending.append(other)

    (flat,), stamp = gate(core_ref, packed.sent, [flat])
    flat = flat + swap(flat, "dp", bits[0])
    work.sent, _ = gate(core_ref, [flat], work.sent)
    for s, other in enumerate(pending):
        packet, outs = settle_rows(s, other, tuple(packed.sent))
        sent.append(packet)
    _, stamp = gate(core_ref, [sent[-1]] if sent else [], [])
    if packed.stages:
        packed.step(stamp - core)
    if packed.stages:
        packed.step(stamp - core)
    other = swap(mine[-1], "tensor", 2)
    _, stamp = gate(core_ref, [other], [])
    ready = [*packed.sent, *(work.receive() if work.stages else [])]
    packet, outs = settle_rows(seqs - 1, other, tuple(ready))
    (flat, *last), stamp = gate(core_ref, [packet], [flat, *sent])
    both = work.finish(stamp - core)
    dproj, dfc = both[:units], both[units:]
    for s, each in enumerate(last):
        outs = place(core_ref, s, swap(each, "tensor", 1), outs)
    if packed.stages:
        packed.received, stamp = gate(core_ref, outs, packed.receive())
    norms = flat[:4, :width]
    norms = norms + swap(norms, "tensor", 1)
    norms = norms + swap(norms, "tensor", 2)
    outs = place(core_ref, seqs - 1, swap(packet, "tensor", 1), outs)
    block_out, input_grad = outs
    packed = packed.finish(stamp - core)
    dqkv = packed[: heads * triple].reshape(heads, triple, width).transpose(2, 0, 1)
    ddense = packed[heads * triple :]

    dfcb, dbias, dbqkv = flat[4, :units], flat[5, :width], flat[6, : heads * triple]
    return (
        block_out,
        input_grad,
        norms[0],
        norms[1],
        norms[2],
        norms[3],
        dqkv,
        dbqkv.reshape(heads, triple),
        ddense,
        dbias,
        dfc,
        dfcb,
        dproj,
        dbias,
    )


def solution(mesh):
    in_specs = (
        P("dp", None),
        P(),
        P(),
        P(),
        P(),
        P(None, "tensor", None),
        P("tensor", None),
        P("tensor", None),
        P(),
        P(None, "tensor"),
        P("tensor"),
        P("tensor", None),
        P(),
        P("dp", None),
    )
    out_specs = (
        P("dp", None),
        P("dp", None),
        P(),
        P(),
        P(),
        P(),
        P(None, "tensor", None),
        P("tensor", None),
        P("tensor", None),
        P(),
        P(None, "tensor"),
        P("tensor"),
        P("tensor", None),
        P(),
    )
    return jax.shard_map(local, mesh=mesh, in_specs=in_specs, out_specs=out_specs, check_vma=False)
```
